256 devices in a mesh: tile: 128 (over z, x, y), pos: 2 (over core).
Axes of the slice: x: 4, y: 4, z: 8, core: 2. Of those that a mesh axis runs over, the one named last changes fastest.
Arguments:
- object_field: float32 [2, 16384, 1024], P(None, 'tile'), may hold values from -10 to 10
- probe_field: float32 [2, 128, 128], replicated, may hold values from -4 to 4
- amplitudes: float32 [128, 2, 32, 128, 128], P('tile', 'pos'), may hold values from 0 to 2
- scan_rows: int32 [128, 2, 32], P('tile', 'pos'), may hold values from 0 to 127
- scan_cols: int32 [128, 2, 32], P('tile', 'pos'), may hold values from 0 to 1023
- live_count: int32 [128, 2], P('tile', 'pos'), may hold values from 8 to 32, as said below
Outputs:
- object_out: float32 [2, 16384, 1024], P(None, 'tile')
- probe_out: float32 [2, 128, 128], replicated
The draws below stay inside these ranges and needn't reach their ends.
Inputs may be any that keep to these rules, and one draw needn't show every extreme that they name: Slot j of device (t, p) holds a scan position exactly when j < live_count[t, p]; some device holds 32.
All inputs are finite; a program needn't handle non-finite values.
Results may differ from the reference program's by a relative error of at most 0.0003.
Values sent between devices are 32-bit elements; how exact they have to be, the bound alone decides.
No kernel may reach another device: no remote copies, remote signals or barrier semaphores. Data moves between devices by JAX's collectives and lax.ppermute only.
A program may use at most 64 MiB of HBM per device.

```python
import jax
import jax.numpy as jnp
from jax import lax

PATCH = 128
STRIP = 128
COLS = 1024
POS_CAP = 32
ITERS = 2
ROWS = 16384
SLOTS = 8192
N_TILE = 128
N_POS = 2


def draw_object_field(key, part):
    row_place = jnp.arange(ROWS, dtype=jnp.float32)
    row_scale = 0.45 * jnp.exp(jnp.log(3.0) * row_place / ROWS)
    key_base, key_rough = jax.random.split(key)
    base_values = jnp.clip(jax.random.normal(key_base, (2, ROWS, COLS), jnp.float32), -5.0, 5.0)
    rough_factor = jnp.exp(jax.random.uniform(key_rough, (2, ROWS, COLS), jnp.float32, -0.35, 0.35))
    return base_values * rough_factor * row_scale[None, :, None]


def draw_live_count(key, part):
    lowest = max(1, POS_CAP // 4)
    spread = max(POS_CAP - lowest, 1)
    raw_draw = jax.random.randint(key, (N_TILE, N_POS), 0, POS_CAP - lowest + 1, dtype=jnp.int32)
    counts = lowest + raw_draw * raw_draw // spread
    counts = jnp.minimum(counts, POS_CAP)
    counts = counts.at[0, 0].set(POS_CAP)
    counts = counts.at[N_TILE - 1, N_POS - 1].set(lowest)
    return counts.astype(jnp.int32)


def touch_ends(result, key, low, top_value):
    longest = result.shape.index(max(result.shape))
    spots = []
    for shift in (0, 1):
        where = [jax.random.randint(jax.random.fold_in(key, axis), (), 0, length) for axis, length in enumerate(result.shape)]
        where[longest] = (where[longest] + shift) % result.shape[longest]
        spots.append(tuple(where))
    return result.at[spots[0]].set(low).at[spots[1]].set(top_value)


def level_of(stream_key, shape, cuts, least, largest):
    loudness, own = 1.0, jax.random.fold_in(stream_key, 6)
    for position, blocks in cuts:
        steps = jnp.exp(jax.random.uniform(jax.random.fold_in(own, position), (blocks,), jnp.float32, least / len(cuts), largest / len(cuts)))
        loudness = loudness * jnp.repeat(steps, shape[position] // blocks).reshape([-1 if axis == position else 1 for axis in range(len(shape))])
    return loudness


def noise(stream_key, extent, scale, bound, held_as=jnp.bfloat16):
    array = jax.random.normal(stream_key, extent, jnp.float32) * scale
    return jnp.minimum(jnp.maximum(array, -bound), bound).astype(held_as)


def setup_inputs(seed: int = 0) -> dict:
    key_of = jax.random.split(jax.random.key(seed), 7)
    return {
        "object_field": draw_object_field(jax.random.fold_in(key_of[6], 71), 0),
        "probe_field": noise(key_of[1], (2, PATCH, PATCH), 0.7, 4.0, jnp.float32),
        "amplitudes": jnp.clip(2.0 * jax.random.uniform(key_of[2], (N_TILE, N_POS, POS_CAP, PATCH, PATCH), jnp.float32) ** level_of(key_of[2], (N_TILE, N_POS, POS_CAP, PATCH, PATCH), ((0, 128), (1, 2)), -0.2, 0.2), 0.0, 2.0),
        "scan_rows": touch_ends(jax.random.randint(key_of[3], (N_TILE, N_POS, POS_CAP), 0, STRIP), jax.random.fold_in(key_of[3], 1), 0, STRIP - 1).astype(jnp.int32),
        "scan_cols": touch_ends(jax.random.randint(key_of[4], (N_TILE, N_POS, POS_CAP), 0, COLS), jax.random.fold_in(key_of[4], 1), 0, COLS - 1).astype(jnp.int32),
        "live_count": draw_live_count(jax.random.fold_in(key_of[6], 71), 0),
    }


MODULUS_FLOOR = 0.2
OBJECT_RELAX = 1.0

def tile_update(extended, probe_field, tile_amps, tile_rows, tile_cols, tile_counts, tile_number):
    zero_index = jnp.zeros((), jnp.int32)
    band_row = (tile_number * STRIP).astype(jnp.int32)
    strip_band = lax.dynamic_slice(extended, (zero_index, band_row, zero_index), (2, 2 * STRIP, COLS + PATCH))
    slot_number = jnp.arange(POS_CAP, dtype=jnp.int32)
    live_mask = (slot_number[None, :] < tile_counts[:, None]).reshape(-1)
    probe_real = probe_field[0]
    probe_imag = probe_field[1]

    def visit_position(state_pair, item_tuple):
        band_sums, probe_sums = state_pair
        amplitude, row_start, col_start, is_live = item_tuple
        corner = (zero_index, row_start.astype(jnp.int32), col_start.astype(jnp.int32))
        patch_wave = lax.dynamic_slice(strip_band, corner, (2, PATCH, PATCH))
        exit_wave = probe_real * patch_wave[0] - probe_imag * patch_wave[1] + 1j * (probe_real * patch_wave[1] + probe_imag * patch_wave[0])
        far_field = jnp.fft.fft2(exit_wave, norm='ortho')
        magnitude = jnp.sqrt(far_field.real ** 2 + far_field.imag ** 2)
        projected = far_field * (amplitude / jnp.maximum(magnitude, MODULUS_FLOOR))
        revised = jnp.fft.ifft2(projected, norm='ortho')
        back_real = revised.real
        back_imag = revised.imag
        object_terms = jnp.stack([probe_real * back_real + probe_imag * back_imag, probe_real * back_imag - probe_imag * back_real, probe_real * probe_real + probe_imag * probe_imag])
        object_terms = jnp.where(is_live, object_terms, 0.0)
        probe_terms = jnp.stack([patch_wave[0] * back_real + patch_wave[1] * back_imag, patch_wave[0] * back_imag - patch_wave[1] * back_real, patch_wave[0] * patch_wave[0] + patch_wave[1] * patch_wave[1]])
        probe_terms = jnp.where(is_live, probe_terms, 0.0)
        current = lax.dynamic_slice(band_sums, corner, (3, PATCH, PATCH))
        band_sums = lax.dynamic_update_slice(band_sums, current + object_terms, corner)
        return ((band_sums, probe_sums + probe_terms), None)
    initial = (jnp.zeros((3, 2 * STRIP, COLS + PATCH), jnp.float32), jnp.zeros((3, PATCH, PATCH), jnp.float32))
    items = (tile_amps.reshape(-1, PATCH, PATCH), tile_rows.reshape(-1), tile_cols.reshape(-1), live_mask)
    finals, unused = lax.scan(visit_position, initial, items)
    return finals

def one_round(object_field, probe_field, amplitudes, scan_rows, scan_cols, live_count):
    extended = jnp.concatenate([object_field, object_field[:, :STRIP]], axis=1)
    extended = jnp.concatenate([extended, extended[:, :, :PATCH]], axis=2)
    tile_numbers = jnp.arange(N_TILE, dtype=jnp.int32)

    def per_tile(item_tuple):
        tile_number, tile_amps, tile_rows, tile_cols, tile_counts = item_tuple
        return tile_update(extended, probe_field, tile_amps, tile_rows, tile_cols, tile_counts, tile_number)
    band_sums, probe_sums = lax.map(per_tile, (tile_numbers, amplitudes, scan_rows, scan_cols, live_count))
    folded = band_sums[..., :COLS].at[..., :PATCH].add(band_sums[..., COLS:])
    strip_sums = folded[:, :, :STRIP] + jnp.roll(folded[:, :, STRIP:], 1, axis=0)
    object_sums = jnp.transpose(strip_sums, (1, 0, 2, 3)).reshape(3, ROWS, COLS)
    object_next = (object_sums[:2] + OBJECT_RELAX * object_field) / (object_sums[2] + OBJECT_RELAX)[None]
    probe_total = lax.optimization_barrier(jnp.sum(probe_sums, axis=0))
    probe_relax = SLOTS / 4.0
    probe_next = (probe_total[:2] + probe_relax * probe_field) / (probe_total[2] + probe_relax)[None]
    return (object_next, probe_next)

def reference(object_field, probe_field, amplitudes, scan_rows, scan_cols, live_count):
    for round_number in range(ITERS):
        object_field, probe_field = one_round(object_field, probe_field, amplitudes, scan_rows, scan_cols, live_count)
    return (object_field, probe_field)
```

```python
import math

import jax
import jax.numpy as jnp
import numpy as np
from jax import lax
from jax.experimental import pallas as pl
from jax.experimental.pallas import tpu as pltpu
from jax.sharding import Mesh
from jax.sharding import PartitionSpec as P

PATCH = 128
STRIP = 128
COLS = 1024
BLOCKS = COLS // PATCH
HALF = BLOCKS // 2
BAND = 2 * STRIP
GROUP = 4
ITERS = 2
TILE = ("tile_0", "tile_1", "tile_2")
MODULUS_FLOOR = 0.2
OBJECT_RELAX = 1.0
ANY = pl.BlockSpec(memory_space=pl.ANY)
SMEM = pl.BlockSpec(memory_space=pltpu.SMEM)
VMEM = pl.BlockSpec(memory_space=pltpu.VMEM)


def swapped(value):
    return lax.ppermute(value, "pos", [(0, 1), (1, 0)])


def from_tile(value, distance):
    count = lax.axis_size(TILE)
    return lax.ppermute(value, TILE, [((i + distance) % count, i) for i in range(count)])


def two_terms(value):
    high = value.astype(jnp.bfloat16)
    low = (value - high.astype(jnp.float32)).astype(jnp.bfloat16)
    return high, low


def dft_tables():
    counter = np.arange(PATCH)
    angle = (counter[:, None] * counter[None, :] % PATCH) * (2.0 * math.pi / PATCH)
    cosine = np.cos(angle) / math.sqrt(PATCH)
    sine = np.sin(angle) / math.sqrt(PATCH)

    def split(table):
        table = table.astype(np.float32)
        high = table.astype(jnp.bfloat16)
        low = (table - high.astype(np.float32)).astype(jnp.bfloat16)
        return high, low

    right, left = [], []
    for sign in (1.0, -1.0):
        high, low = split(np.block([[cosine, -sign * sine], [sign * sine, cosine]]))
        right.append(np.concatenate([high, high, low], axis=0))
        high, low = split(np.block([[cosine, sign * sine], [-sign * sine, cosine]]))
        left.append(np.concatenate([high, high, low], axis=1))
    return jnp.asarray(np.stack(right)), jnp.asarray(np.stack(left))


def times_right(real, imag, table):
    stacked = jnp.concatenate(
        [jnp.concatenate([r, i], axis=1) for r, i in zip(real, imag)], axis=0
    )
    high, low = two_terms(stacked)
    wide = jnp.concatenate([high, low, high], axis=1)
    out = jnp.dot(wide, table, preferred_element_type=jnp.float32)
    return (
        [out[k * PATCH : (k + 1) * PATCH, :PATCH] for k in range(len(real))],
        [out[k * PATCH : (k + 1) * PATCH, PATCH:] for k in range(len(real))],
    )


def times_left(real, imag, table):
    stacked = jnp.concatenate(
        [jnp.concatenate(real, axis=1), jnp.concatenate(imag, axis=1)], axis=0
    )
    high, low = two_terms(stacked)
    tall = jnp.concatenate([high, low, high], axis=0)
    out = jnp.dot(table, tall, preferred_element_type=jnp.float32)
    return (
        [out[:PATCH, k * PATCH : (k + 1) * PATCH] for k in range(len(real))],
        [out[PATCH:, k * PATCH : (k + 1) * PATCH] for k in range(len(real))],
    )


def column_place(col, own_first):
    block = col // PATCH
    near = block ^ own_first
    far = ((block + 1) % BLOCKS) ^ own_first
    return near, far, col % PATCH


def positions_kernel(
    from_strips,
    core_ref,
    rows_ref,
    cols_ref,
    live_ref,
    probe_ref,
    amps_ref,
    right_ref,
    left_ref,
    first_ref,
    mine_ref,
    other_ref,
    keep_up_ref,
    keep_low_ref,
    give_up_ref,
    give_low_ref,
    probe_sums_ref,
    band,
    sums,
    sems,
):
    own_first = core_ref[0] * HALF
    copies = []
    if from_strips:
        for k in range(BLOCKS):
            start = pl.multiple_of((k ^ own_first) * PATCH, PATCH)
            copies.append((first_ref.at[:, :, pl.ds(start, PATCH)], band.at[:, k, :STRIP, :]))
        copies.append((mine_ref, band.at[:, :HALF, STRIP:, :]))
        copies.append((other_ref, band.at[:, HALF:, STRIP:, :]))
    else:
        copies.append((mine_ref, band.at[:, :HALF]))
        copies.append((other_ref, band.at[:, HALF:]))
    started = [pltpu.make_async_copy(a, b, sems.at[n]) for n, (a, b) in enumerate(copies)]
    for copy in started:
        copy.start()
    sums[...] = jnp.zeros_like(sums)
    probe_sums_ref[...] = jnp.zeros_like(probe_sums_ref)
    for copy in started:
        copy.wait()
    live = live_ref[0]
    lane = lax.broadcasted_iota(jnp.int32, (PATCH, PATCH), 1)

    def visit(step, carry):
        slots = [step * GROUP + k for k in range(GROUP)]
        places = [column_place(cols_ref[s], own_first) for s in slots]
        rows = [rows_ref[s] for s in slots]
        alive = [s < live for s in slots]
        probe_real = probe_ref[0]
        probe_imag = probe_ref[1]
        patches = []
        exits = []
        for (near, far, shift), row in zip(places, rows):
            back = (PATCH - shift) % PATCH
            patch = []
            for plane in range(2):
                a = band[plane, near, pl.ds(row, PATCH), :]
                b = band[plane, far, pl.ds(row, PATCH), :]
                patch.append(pltpu.roll(jnp.where(lane >= shift, a, b), back, 1))
            patches.append(patch)
            exits.append(
                (
                    probe_real * patch[0] - probe_imag * patch[1],
                    probe_real * patch[1] + probe_imag * patch[0],
                )
            )
        revised = []
        for pair in range(0, GROUP, 2):
            real = [exits[pair + k][0] for k in range(2)]
            imag = [exits[pair + k][1] for k in range(2)]
            real, imag = times_right(real, imag, right_ref[0])
            real, imag = times_left(real, imag, left_ref[0])
            for k in range(2):
                power = real[k] * real[k] + imag[k] * imag[k]
                ratio = amps_ref[slots[pair + k]] * lax.rsqrt(
                    jnp.maximum(power, MODULUS_FLOOR * MODULUS_FLOOR)
                )
                real[k] = real[k] * ratio
                imag[k] = imag[k] * ratio
            real, imag = times_left(real, imag, left_ref[1])
            real, imag = times_right(real, imag, right_ref[1])
            revised.extend(zip(real, imag))
        totals = [probe_sums_ref[plane] for plane in range(3)]
        for k in range(GROUP):
            back_real = jnp.where(alive[k], revised[k][0], 0.0)
            back_imag = jnp.where(alive[k], revised[k][1], 0.0)
            patch_real = jnp.where(alive[k], patches[k][0], 0.0)
            patch_imag = jnp.where(alive[k], patches[k][1], 0.0)
            totals[0] += patch_real * back_real + patch_imag * back_imag
            totals[1] += patch_real * back_imag - patch_imag * back_real
            totals[2] += patch_real * patch_real + patch_imag * patch_imag
            near, far, shift = places[k]
            terms = (
                probe_real * back_real + probe_imag * back_imag,
                probe_real * back_imag - probe_imag * back_real,
            )
            for plane in range(2):
                turned = pltpu.roll(terms[plane], shift, 1)
                inside = lane >= shift
                sums[plane, near, pl.ds(rows[k], PATCH), :] += jnp.where(inside, turned, 0.0)
                sums[plane, far, pl.ds(rows[k], PATCH), :] += jnp.where(inside, 0.0, turned)
        for plane in range(3):
            probe_sums_ref[plane] = totals[plane]
        return carry

    lax.fori_loop(0, (live + GROUP - 1) // GROUP, visit, 0)
    outs = (
        (sums.at[:, :HALF, :STRIP, :], keep_up_ref),
        (sums.at[:, :HALF, STRIP:, :], keep_low_ref),
        (sums.at[:, HALF:, :STRIP, :], give_up_ref),
        (sums.at[:, HALF:, STRIP:, :], give_low_ref),
    )
    started = [pltpu.make_async_copy(a, b, sems.at[n]) for n, (a, b) in enumerate(outs)]
    for copy in started:
        copy.start()
    for copy in started:
        copy.wait()


def run_positions(scalars, probe, amps, tables, first, mine, other):
    from_strips = first is not None
    quarter = jax.ShapeDtypeStruct((2, HALF, STRIP, PATCH), jnp.float32)

    def kernel(*refs):
        if from_strips:
            positions_kernel(True, *refs)
        else:
            positions_kernel(False, *refs[:8], None, *refs[8:])

    pieces = (first, mine, other) if from_strips else (mine, other)
    return pl.pallas_call(
        kernel,
        out_shape=(quarter,) * 4 + (jax.ShapeDtypeStruct((3, PATCH, PATCH), jnp.float32),),
        in_specs=[SMEM] * 4 + [VMEM] * 4 + [ANY] * len(pieces),
        out_specs=(ANY,) * 4 + (VMEM,),
        scratch_shapes=[
            pltpu.VMEM((2, BLOCKS, BAND, PATCH), jnp.float32),
            pltpu.VMEM((2, BLOCKS, BAND, PATCH), jnp.float32),
            pltpu.SemaphoreType.DMA((BLOCKS + 2,)),
        ],
        compiler_params=pltpu.CompilerParams(vmem_limit_bytes=40 * 2**20),
        cost_estimate=pl.CostEstimate(
            flops=13 * 10**9, bytes_accessed=8 * 2**20, transcendentals=2**19
        ),
        name="positions",
    )(*scalars, probe, amps, *tables, *pieces)


def weights_kernel(sources, core_ref, meta_ref, probe_ref, out_ref, total, power):
    own_first = core_ref[0] * HALF
    total[...] = jnp.zeros_like(total)
    power[...] = probe_ref[0] * probe_ref[0] + probe_ref[1] * probe_ref[1]
    lane = lax.broadcasted_iota(jnp.int32, (PATCH, PATCH), 1)
    slots = (meta_ref.shape[1] - 2) // 2
    for source in range(sources):
        for core in range(2):
            line = source * 2 + core

            def visit(slot, carry, line=line, source=source):
                row = meta_ref[line, slot] + source * STRIP
                near, far, shift = column_place(meta_ref[line, slots + slot], own_first)

                @pl.when(near < HALF)
                def _():
                    turned = pltpu.roll(power[...], shift, 1)
                    total[near, pl.ds(row, PATCH), :] += jnp.where(lane >= shift, turned, 0.0)

                @pl.when(far < HALF)
                def _():
                    turned = pltpu.roll(power[...], shift, 1)
                    total[far, pl.ds(row, PATCH), :] += jnp.where(lane >= shift, 0.0, turned)

                return carry

            lax.fori_loop(0, meta_ref[line, 2 * slots], visit, 0)
    height = out_ref.shape[1]
    out_ref[...] = total[:, STRIP : STRIP + height, :] + OBJECT_RELAX


def run_weights(core, meta, probe, sources):
    height = (sources - 1) * STRIP

    def kernel(*refs):
        weights_kernel(sources, *refs)

    return pl.pallas_call(
        kernel,
        out_shape=jax.ShapeDtypeStruct((HALF, height, PATCH), jnp.float32),
        in_specs=[SMEM, SMEM, VMEM],
        out_specs=VMEM,
        scratch_shapes=[
            pltpu.VMEM((HALF, (sources + 1) * STRIP, PATCH), jnp.float32),
            pltpu.VMEM((PATCH, PATCH), jnp.float32),
        ],
        compiler_params=pltpu.CompilerParams(vmem_limit_bytes=16 * 2**20),
        cost_estimate=pl.CostEstimate(
            flops=4 * 10**9, bytes_accessed=2 * 2**20, transcendentals=0
        ),
        name="weights",
    )(core, meta, probe)


def probe_sum_everywhere(value):
    core = lax.axis_index("pos")
    lines = value.reshape(2, -1, PATCH)
    mine = lax.dynamic_index_in_dim(lines, core, 0, False)
    other = lax.dynamic_index_in_dim(lines, 1 - core, 0, False)
    part = mine + swapped(other)
    for axis in TILE[::-1]:
        count = lax.axis_size(axis)
        stride = 1
        while stride < count:
            fan = 4 if count % (stride * 4) == 0 else 2
            part = shifts_among(part, axis, stride, fan)
            stride *= fan
    other = swapped(part)
    low = jnp.where(core == 0, part, other)
    high = jnp.where(core == 0, other, part)
    return jnp.concatenate([low, high]).reshape(value.shape)


def shifts_among(value, axis, stride, fan):
    count = lax.axis_size(axis)
    total = value
    for step in range(1, fan):
        route = []
        for i in range(count):
            place = i // stride % fan
            route.append((i, i + ((place + step) % fan - place) * stride))
        total = total + lax.ppermute(value, axis, route)
    return total


def halves_of(value, core):
    lines = value.reshape(*value.shape[:2], 2, HALF, PATCH)
    mine = lax.dynamic_index_in_dim(lines, core, 2, False)
    return mine.transpose(0, 2, 1, 3)


def on_device(object_field, probe_field, amplitudes, scan_rows, scan_cols, live_count):
    tables = dft_tables()
    core = lax.axis_index("pos")
    core_line = core.reshape(1).astype(jnp.int32)
    amps, rows, cols, live = (
        amplitudes[0, 0],
        scan_rows[0, 0],
        scan_cols[0, 0],
        live_count[0],
    )
    scalars = (core_line, rows, cols, live)
    probe_relax = amps.shape[0] * lax.axis_size(TILE) * lax.axis_size("pos") / 4.0
    own_half = halves_of(object_field, core)
    halo = from_tile(own_half, 1)
    meta = jnp.concatenate([rows, cols, live, live])[None]
    meta = jnp.concatenate([meta, swapped(meta)])
    meta = jnp.concatenate([from_tile(meta, -1), meta, from_tile(meta, 1)])
    halo_other = swapped(halo)
    weight = run_weights(core_line, meta, probe_field, 3)
    up, low, give_up, give_low, probe_sums = run_positions(
        scalars, probe_field, amps, tables, object_field, halo, halo_other
    )

    def next_probe(sums, probe):
        total = probe_sum_everywhere(sums)
        return (total[:2] + probe_relax * probe) / (total[2] + probe_relax)[None]

    low = low + swapped(give_low)
    up = up + swapped(give_up)
    above = from_tile(low, -1)
    below = from_tile(up, 1)
    probe_field = next_probe(probe_sums, probe_field)
    up = (up + above + OBJECT_RELAX * own_half) / weight[:, :STRIP]
    low = (low + below + OBJECT_RELAX * halo) / weight[:, STRIP:]
    mine = jnp.concatenate([up, low], axis=2)
    other = swapped(mine)
    own_half = up
    weight = run_weights(core_line, meta[:4], probe_field, 2)
    up, low, give_up, give_low, probe_sums = run_positions(
        scalars, probe_field, amps, tables, None, mine, other
    )
    low = low + swapped(give_low)
    up = up + swapped(give_up)
    above = from_tile(low, -1)
    probe_out = next_probe(probe_sums, probe_field)
    mine = (up + above + OBJECT_RELAX * own_half) / weight
    other = swapped(mine)
    left = jnp.where(core == 0, mine, other)
    right = jnp.where(core == 0, other, mine)
    object_out = jnp.concatenate([left, right], axis=1).transpose(0, 2, 1, 3)
    return object_out.reshape(object_field.shape), probe_out


def torus_of(mesh):
    shape = (mesh.shape["tile"],)
    shape = (8, 4, 4) if shape == (128,) else (1, 1, *shape)
    return Mesh(mesh.devices.reshape(*shape, mesh.shape["pos"]), (*TILE, "pos"))


def solution(mesh):
    return jax.shard_map(
        on_device,
        mesh=torus_of(mesh),
        in_specs=(
            P(None, TILE, None),
            P(),
            P(TILE, "pos", None, None, None),
            P(TILE, "pos", None),
            P(TILE, "pos", None),
            P(TILE, "pos"),
        ),
        out_specs=(P(None, TILE, None), P()),
        check_vma=False,
    )
```

```python
import math

import jax
import jax.numpy as jnp
import numpy as np
from jax import lax
from jax.experimental import pallas as pl
from jax.experimental.pallas import tpu as pltpu
from jax.sharding import Mesh
from jax.sharding import PartitionSpec as P

PATCH = 128
STRIP = 128
COLS = 1024
BLOCKS = COLS // PATCH
HALF = BLOCKS // 2
BAND = 2 * STRIP
GROUP = 4
ITERS = 2
TILE = ("tile_0", "tile_1", "tile_2")
MODULUS_FLOOR = 0.2
OBJECT_RELAX = 1.0
ANY = pl.BlockSpec(memory_space=pl.ANY)
SMEM = pl.BlockSpec(memory_space=pltpu.SMEM)
VMEM = pl.BlockSpec(memory_space=pltpu.VMEM)


def swapped(value):
    return lax.ppermute(value, "pos", [(0, 1), (1, 0)])


def from_tile(value, distance):
    count = lax.axis_size(TILE)
    return lax.ppermute(value, TILE, [((i + distance) % count, i) for i in range(count)])


def two_terms(value):
    high = value.astype(jnp.bfloat16)
    low = (value - high.astype(jnp.float32)).astype(jnp.bfloat16)
    return high, low


def dft_tables():
    counter = np.arange(PATCH)
    angle = (counter[:, None] * counter[None, :] % PATCH) * (2.0 * math.pi / PATCH)
    cosine = np.cos(angle) / math.sqrt(PATCH)
    sine = np.sin(angle) / math.sqrt(PATCH)
    tables = []
    for sign in (1.0, -1.0):
        for turn in (1.0, -1.0):
            cross = sign * turn * sine
            table = np.block([[cosine, -cross], [cross, cosine]]).astype(np.float32)
            high = table.astype(jnp.bfloat16)
            tables += [high, (table - high.astype(np.float32)).astype(jnp.bfloat16)]
    return jnp.asarray(np.stack(tables))


def times_right(real, imag, high_table, low_table):
    stacked = jnp.concatenate(
        [jnp.concatenate([r, i], axis=1) for r, i in zip(real, imag)], axis=0
    )
    high, low = two_terms(stacked)
    wide = jnp.concatenate([high, low, high], axis=1)
    table = jnp.concatenate([high_table, high_table, low_table], axis=0)
    out = jnp.dot(wide, table, preferred_element_type=jnp.float32)
    return (
        [out[k * PATCH : (k + 1) * PATCH, :PATCH] for k in range(len(real))],
        [out[k * PATCH : (k + 1) * PATCH, PATCH:] for k in range(len(real))],
    )


def times_left(real, imag, high_table, low_table):
    stacked = jnp.concatenate(
        [jnp.concatenate(real, axis=1), jnp.concatenate(imag, axis=1)], axis=0
    )
    high, low = two_terms(stacked)
    tall = jnp.concatenate([high, low, high], axis=0)
    table = jnp.concatenate([high_table, high_table, low_table], axis=1)
    out = jnp.dot(table, tall, preferred_element_type=jnp.float32)
    return (
        [out[:PATCH, k * PATCH : (k + 1) * PATCH] for k in range(len(real))],
        [out[PATCH:, k * PATCH : (k + 1) * PATCH] for k in range(len(real))],
    )


def column_place(col, own_first):
    block = col // PATCH
    near = block ^ own_first
    far = ((block + 1) % BLOCKS) ^ own_first
    return near, far, col % PATCH


def positions_kernel(
    from_strips,
    core_ref,
    rows_ref,
    cols_ref,
    live_ref,
    probe_ref,
    amps_hbm,
    tables_hbm,
    first_ref,
    mine_ref,
    other_ref,
    keep_up_ref,
    keep_low_ref,
    give_up_ref,
    give_low_ref,
    probe_sums_ref,
    band,
    sums,
    amps_ref,
    tables,
    sems,
    amp_sems,
):
    own_first = core_ref[0] * HALF
    groups = amps_ref.shape[0] // GROUP

    def amp_copy(group):
        place = pl.ds(group * GROUP, GROUP)
        return pltpu.make_async_copy(amps_hbm.at[place], amps_ref.at[place], amp_sems.at[group])

    copies = [(tables_hbm, tables)]
    if from_strips:
        for k in range(BLOCKS):
            start = pl.multiple_of((k ^ own_first) * PATCH, PATCH)
            copies.append((first_ref.at[:, :, pl.ds(start, PATCH)], band.at[:, k, :STRIP, :]))
            half = mine_ref if k < HALF else other_ref
            columns = pl.ds(k % HALF * PATCH, PATCH)
            copies.append((half.at[:, :, columns], band.at[:, k, STRIP:, :]))
    else:
        copies.append((mine_ref, band.at[:, :HALF]))
        copies.append((other_ref, band.at[:, HALF:]))
    started = [pltpu.make_async_copy(a, b, sems.at[n]) for n, (a, b) in enumerate(copies)]
    for copy in started:
        copy.start()
    for group in range(groups):
        amp_copy(group).start()
    sums[...] = jnp.zeros_like(sums)
    probe_sums_ref[...] = jnp.zeros_like(probe_sums_ref)
    for copy in started:
        copy.wait()
    live = live_ref[0]
    lane = lax.broadcasted_iota(jnp.int32, (PATCH, PATCH), 1)

    def visit(step, carry):
        amp_copy(step).wait()
        slots = [step * GROUP + k for k in range(GROUP)]
        places = [column_place(cols_ref[s], own_first) for s in slots]
        rows = [rows_ref[s] for s in slots]
        alive = [s < live for s in slots]
        probe_real = probe_ref[0]
        probe_imag = probe_ref[1]
        patches = []
        exits = []
        for (near, far, shift), row in zip(places, rows):
            back = (PATCH - shift) % PATCH
            patch = []
            for plane in range(2):
                a = band[plane, near, pl.ds(row, PATCH), :]
                b = band[plane, far, pl.ds(row, PATCH), :]
                patch.append(pltpu.roll(jnp.where(lane >= shift, a, b), back, 1))
            patches.append(patch)
            exits.append(
                (
                    probe_real * patch[0] - probe_imag * patch[1],
                    probe_real * patch[1] + probe_imag * patch[0],
                )
            )
        revised = []
        for pair in range(0, GROUP, 2):
            real = [exits[pair + k][0] for k in range(2)]
            imag = [exits[pair + k][1] for k in range(2)]
            real, imag = times_right(real, imag, tables[0], tables[1])
            real, imag = times_left(real, imag, tables[2], tables[3])
            for k in range(2):
                power = real[k] * real[k] + imag[k] * imag[k]
                ratio = amps_ref[slots[pair + k]] * lax.rsqrt(
                    jnp.maximum(power, MODULUS_FLOOR * MODULUS_FLOOR)
                )
                real[k] = real[k] * ratio
                imag[k] = imag[k] * ratio
            real, imag = times_left(real, imag, tables[6], tables[7])
            real, imag = times_right(real, imag, tables[4], tables[5])
            revised.extend(zip(real, imag))
        totals = [probe_sums_ref[plane] for plane in range(3)]
        probe_power = probe_real * probe_real + probe_imag * probe_imag
        for k in range(GROUP):
            back_real = jnp.where(alive[k], revised[k][0], 0.0)
            back_imag = jnp.where(alive[k], revised[k][1], 0.0)
            patch_real = jnp.where(alive[k], patches[k][0], 0.0)
            patch_imag = jnp.where(alive[k], patches[k][1], 0.0)
            totals[0] += patch_real * back_real + patch_imag * back_imag
            totals[1] += patch_real * back_imag - patch_imag * back_real
            totals[2] += patch_real * patch_real + patch_imag * patch_imag
            near, far, shift = places[k]
            terms = (
                probe_real * back_real + probe_imag * back_imag,
                probe_real * back_imag - probe_imag * back_real,
                jnp.where(alive[k], probe_power, 0.0),
            )
            for plane in range(3):
                turned = pltpu.roll(terms[plane], shift, 1)
                inside = lane >= shift
                sums[plane, near, pl.ds(rows[k], PATCH), :] += jnp.where(inside, turned, 0.0)
                sums[plane, far, pl.ds(rows[k], PATCH), :] += jnp.where(inside, 0.0, turned)
        for plane in range(3):
            probe_sums_ref[plane] = totals[plane]
        return carry

    def skip(step, carry):
        amp_copy(step).wait()
        return carry

    steps = (live + GROUP - 1) // GROUP
    lax.fori_loop(0, steps, visit, 0)
    outs = (
        (sums.at[:, HALF:, STRIP:, :], give_low_ref),
        (sums.at[:, HALF:, :STRIP, :], give_up_ref),
        (sums.at[:, :HALF, STRIP:, :], keep_low_ref),
        (sums.at[:, :HALF, :STRIP, :], keep_up_ref),
    )
    started = [pltpu.make_async_copy(a, b, sems.at[n]) for n, (a, b) in enumerate(outs)]
    for copy in started:
        copy.start()
    lax.fori_loop(steps, groups, skip, 0)
    for copy in started:
        copy.wait()


def run_positions(scalars, probe, amps, tables, first, mine, other):
    from_strips = first is not None
    quarter = jax.ShapeDtypeStruct((3, HALF, STRIP, PATCH), jnp.float32)

    def kernel(*refs):
        if from_strips:
            positions_kernel(True, *refs)
        else:
            positions_kernel(False, *refs[:7], None, *refs[7:])

    pieces = (first, mine, other) if from_strips else (mine, other)
    return pl.pallas_call(
        kernel,
        out_shape=(quarter,) * 4 + (jax.ShapeDtypeStruct((3, PATCH, PATCH), jnp.float32),),
        in_specs=[SMEM] * 4 + [VMEM] + [ANY] * (2 + len(pieces)),
        out_specs=(ANY,) * 4 + (VMEM,),
        scratch_shapes=[
            pltpu.VMEM((2, BLOCKS, BAND, PATCH), jnp.float32),
            pltpu.VMEM((3, BLOCKS, BAND, PATCH), jnp.float32),
            pltpu.VMEM(amps.shape, jnp.float32),
            pltpu.VMEM(tables.shape, tables.dtype),
            pltpu.SemaphoreType.DMA((2 * BLOCKS + 1,)),
            pltpu.SemaphoreType.DMA((amps.shape[0] // GROUP,)),
        ],
        compiler_params=pltpu.CompilerParams(vmem_limit_bytes=40 * 2**20),
        cost_estimate=pl.CostEstimate(
            flops=13 * 10**9, bytes_accessed=8 * 2**20, transcendentals=2**19
        ),
        name="positions",
    )(*scalars, probe, amps, tables, *pieces)


def probe_sum_everywhere(value):
    core = lax.axis_index("pos")
    lines = value.reshape(2, -1, PATCH)
    mine = lax.dynamic_index_in_dim(lines, core, 0, False)
    other = lax.dynamic_index_in_dim(lines, 1 - core, 0, False)
    part = mine + swapped(other)
    for axis in TILE[::-1]:
        count = lax.axis_size(axis)
        stride = 1
        while stride < count:
            fan = 4 if count % (stride * 4) == 0 else 2
            part = shifts_among(part, axis, stride, fan)
            stride *= fan
    other = swapped(part)
    low = jnp.where(core == 0, part, other)
    high = jnp.where(core == 0, other, part)
    return jnp.concatenate([low, high]).reshape(value.shape)


def shifts_among(value, axis, stride, fan):
    count = lax.axis_size(axis)
    total = value
    for step in range(1, fan):
        route = []
        for i in range(count):
            place = i // stride % fan
            route.append((i, i + ((place + step) % fan - place) * stride))
        total = total + lax.ppermute(value, axis, route)
    return total


def in_blocks(value):
    lines = value.reshape(*value.shape[:2], HALF, PATCH)
    return lines.transpose(0, 2, 1, 3)


def on_device(object_field, probe_field, amplitudes, scan_rows, scan_cols, live_count):
    tables = dft_tables()
    core = lax.axis_index("pos")
    amps = amplitudes[0, 0]
    scalars = (
        core.reshape(1).astype(jnp.int32),
        scan_rows[0, 0],
        scan_cols[0, 0],
        live_count[0],
    )
    probe_relax = amps.shape[0] * lax.axis_size(TILE) * lax.axis_size("pos") / 4.0
    own_half = lax.dynamic_slice_in_dim(object_field, core * (COLS // 2), COLS // 2, 2)
    halo = from_tile(own_half, 1)
    halo_other = swapped(halo)
    up, low, give_up, give_low, probe_sums = run_positions(
        scalars, probe_field, amps, tables, object_field, halo, halo_other
    )

    def next_probe(sums, probe):
        total = probe_sum_everywhere(sums)
        return (total[:2] + probe_relax * probe) / (total[2] + probe_relax)[None]

    def updated(sums, field):
        return (sums[:2] + OBJECT_RELAX * field) / (sums[2] + OBJECT_RELAX)[None]

    low = low + swapped(give_low)
    up = up + swapped(give_up)
    above = from_tile(low, -1)
    below = from_tile(up, 1)
    probe_field = next_probe(probe_sums, probe_field)
    own_half = updated(up + above, in_blocks(own_half))
    mine = jnp.concatenate([own_half, updated(low + below, in_blocks(halo))], axis=2)
    other = swapped(mine)
    up, low, give_up, give_low, probe_sums = run_positions(
        scalars, probe_field, amps, tables, None, mine, other
    )
    low = low + swapped(give_low)
    up = up + swapped(give_up)
    above = from_tile(low, -1)
    probe_out = next_probe(probe_sums, probe_field)
    mine = updated(up + above, own_half).transpose(0, 2, 1, 3).reshape(2, STRIP, COLS // 2)
    other = swapped(mine)
    left = jnp.where(core == 0, mine, other)
    right = jnp.where(core == 0, other, mine)
    return jnp.concatenate([left, right], axis=2), probe_out


def torus_of(mesh):
    shape = (mesh.shape["tile"],)
    shape = (8, 4, 4) if shape == (128,) else (1, 1, *shape)
    return Mesh(mesh.devices.reshape(*shape, mesh.shape["pos"]), (*TILE, "pos"))


def solution(mesh):
    return jax.shard_map(
        on_device,
        mesh=torus_of(mesh),
        in_specs=(
            P(None, TILE, None),
            P(),
            P(TILE, "pos", None, None, None),
            P(TILE, "pos", None),
            P(TILE, "pos", None),
            P(TILE, "pos"),
        ),
        out_specs=(P(None, TILE, None), P()),
        check_vma=False,
    )
```

```python
import math

import jax
import jax.numpy as jnp
import numpy as np
from jax import lax
from jax.experimental import pallas as pl
from jax.experimental.pallas import tpu as pltpu
from jax.sharding import Mesh
from jax.sharding import PartitionSpec as P

PATCH = 128
STRIP = 128
COLS = 1024
BLOCKS = COLS // PATCH
HALF = BLOCKS // 2
BAND = 2 * STRIP
GROUP = 8
ITERS = 2
TILE = ("tile_0", "tile_1", "tile_2")
MODULUS_FLOOR = 0.2
OBJECT_RELAX = 1.0
ANY = pl.BlockSpec(memory_space=pl.ANY)
VMEM = pl.BlockSpec(memory_space=pltpu.VMEM)


def swapped(value):
    return lax.ppermute(value, "pos", [(0, 1), (1, 0)])


def from_tile(value, distance):
    count = lax.axis_size(TILE)
    return lax.ppermute(value, TILE, [((i + distance) % count, i) for i in range(count)])


def two_terms(value):
    high = value.astype(jnp.bfloat16)
    low = (value - high.astype(jnp.float32)).astype(jnp.bfloat16)
    return high, low


def dft_tables():
    counter = np.arange(PATCH)
    angle = (counter[:, None] * counter[None, :] % PATCH) * (2.0 * math.pi / PATCH)
    cosine = np.cos(angle) / math.sqrt(PATCH)
    sine = np.sin(angle) / math.sqrt(PATCH)
    tables = []
    for sign in (1.0, -1.0):
        for turn in (1.0, -1.0):
            cross = sign * turn * sine
            table = np.block([[cosine, -cross], [cross, cosine]]).astype(np.float32)
            high = table.astype(jnp.bfloat16)
            tables += [high, (table - high.astype(np.float32)).astype(jnp.bfloat16)]
    return jnp.asarray(np.stack(tables))


def times_right(real, imag, high_table, low_table):
    stacked = jnp.concatenate(
        [jnp.concatenate([r, i], axis=1) for r, i in zip(real, imag)], axis=0
    )
    high, low = two_terms(stacked)
    wide = jnp.concatenate([high, low, high], axis=1)
    table = jnp.concatenate([high_table, high_table, low_table], axis=0)
    out = jnp.dot(wide, table, preferred_element_type=jnp.float32)
    return (
        [out[k * PATCH : (k + 1) * PATCH, :PATCH] for k in range(len(real))],
        [out[k * PATCH : (k + 1) * PATCH, PATCH:] for k in range(len(real))],
    )


def times_left(real, imag, high_table, low_table):
    stacked = jnp.concatenate(
        [jnp.concatenate(real, axis=1), jnp.concatenate(imag, axis=1)], axis=0
    )
    high, low = two_terms(stacked)
    tall = jnp.concatenate([high, low, high], axis=0)
    table = jnp.concatenate([high_table, high_table, low_table], axis=1)
    out = jnp.dot(table, tall, preferred_element_type=jnp.float32)
    return (
        [out[:PATCH, k * PATCH : (k + 1) * PATCH] for k in range(len(real))],
        [out[PATCH:, k * PATCH : (k + 1) * PATCH] for k in range(len(real))],
    )


def column_place(col, own_first):
    block = col // PATCH
    near = block ^ own_first
    far = ((block + 1) % BLOCKS) ^ own_first
    return near, far, col % PATCH


def positions_kernel(
    from_strips,
    scalars_hbm,
    probe_ref,
    amps_hbm,
    tables_hbm,
    first_ref,
    mine_ref,
    other_ref,
    keep_up_ref,
    keep_low_ref,
    give_up_ref,
    give_low_ref,
    probe_sums_ref,
    band,
    sums,
    amps_ref,
    tables,
    scalars,
    sems,
    amp_sems,
):
    groups = amps_ref.shape[0] // GROUP
    fetch = pltpu.make_async_copy(scalars_hbm, scalars, sems.at[2 * BLOCKS + 1])
    fetch.start()

    def amp_copy(group):
        place = pl.ds(group * GROUP, GROUP)
        return pltpu.make_async_copy(amps_hbm.at[place], amps_ref.at[place], amp_sems.at[group])

    for group in range(groups):
        amp_copy(group).start()
    sums[...] = jnp.zeros_like(sums)
    probe_sums_ref[...] = jnp.zeros_like(probe_sums_ref)
    fetch.wait()
    own_first = scalars[2, 1] * HALF
    copies = [(tables_hbm, tables)]
    if from_strips:
        for k in range(BLOCKS):
            start = pl.multiple_of((k ^ own_first) * PATCH, PATCH)
            copies.append((first_ref.at[:, :, pl.ds(start, PATCH)], band.at[:, k, :STRIP, :]))
            half = mine_ref if k < HALF else other_ref
            columns = pl.ds(k % HALF * PATCH, PATCH)
            copies.append((half.at[:, :, columns], band.at[:, k, STRIP:, :]))
    else:
        copies.append((mine_ref, band.at[:, :HALF]))
        copies.append((other_ref, band.at[:, HALF:]))
    started = [pltpu.make_async_copy(a, b, sems.at[n]) for n, (a, b) in enumerate(copies)]
    for copy in started:
        copy.start()
    for copy in started:
        copy.wait()
    live = scalars[2, 0]
    lane = lax.broadcasted_iota(jnp.int32, (PATCH, PATCH), 1)

    def visit(step, carry):
        amp_copy(step).wait()
        slots = [step * GROUP + k for k in range(GROUP)]
        places = [column_place(scalars[1, s], own_first) for s in slots]
        rows = [scalars[0, s] for s in slots]
        patches = {}
        waves = {}

        def cut(pair):
            probe_real, probe_imag = probe_ref[0], probe_ref[1]
            real, imag = [], []
            for k in (2 * pair, 2 * pair + 1):
                near, far, shift = places[k]
                back = (PATCH - shift) % PATCH
                patch = []
                for plane in range(2):
                    a = band[plane, near, pl.ds(rows[k], PATCH), :]
                    b = band[plane, far, pl.ds(rows[k], PATCH), :]
                    patch.append(pltpu.roll(jnp.where(lane >= shift, a, b), back, 1))
                patches[k] = patch
                real.append(probe_real * patch[0] - probe_imag * patch[1])
                imag.append(probe_real * patch[1] + probe_imag * patch[0])
            waves[pair] = (real, imag)

        def rescale(pair):
            real, imag = waves[pair]
            for k in range(2):
                slot = slots[2 * pair + k]
                power = real[k] * real[k] + imag[k] * imag[k]
                ratio = jnp.where(slot < live, amps_ref[slot], 0.0) * lax.rsqrt(
                    jnp.maximum(power, MODULUS_FLOOR * MODULUS_FLOOR)
                )
                real[k] = real[k] * ratio
                imag[k] = imag[k] * ratio

        def right(pair, table):
            waves[pair] = times_right(*waves[pair], tables[table], tables[table + 1])

        def left(pair, table):
            waves[pair] = times_left(*waves[pair], tables[table], tables[table + 1])

        def collect(pair):
            probe_real, probe_imag = probe_ref[0], probe_ref[1]
            probe_power = probe_real * probe_real + probe_imag * probe_imag
            totals = [0.0, 0.0, 0.0]
            for back_real, back_imag, k in zip(*waves[pair], (2 * pair, 2 * pair + 1)):
                alive = slots[k] < live
                patch_real, patch_imag = patches[k]
                patch_power = patch_real * patch_real + patch_imag * patch_imag
                totals[0] += patch_real * back_real + patch_imag * back_imag
                totals[1] += patch_real * back_imag - patch_imag * back_real
                totals[2] += jnp.where(alive, patch_power, 0.0)
                near, far, shift = places[k]
                terms = (
                    probe_real * back_real + probe_imag * back_imag,
                    probe_real * back_imag - probe_imag * back_real,
                    jnp.where(alive, probe_power, 0.0),
                )
                inside = lane >= shift
                for plane in range(3):
                    turned = pltpu.roll(terms[plane], shift, 1)
                    sums[plane, near, pl.ds(rows[k], PATCH), :] += jnp.where(inside, turned, 0.0)
                    sums[plane, far, pl.ds(rows[k], PATCH), :] += jnp.where(inside, 0.0, turned)
            for plane in range(3):
                probe_sums_ref[plane] += totals[plane]

        stages = (
            cut,
            lambda pair: right(pair, 0),
            lambda pair: left(pair, 2),
            rescale,
            lambda pair: left(pair, 6),
            lambda pair: right(pair, 4),
            collect,
        )
        pairs = GROUP // 2
        for stage in stages:
            for pair in range(pairs):
                stage(pair)
        return carry

    def skip(step, carry):
        amp_copy(step).wait()
        return carry

    steps = (live + GROUP - 1) // GROUP
    lax.fori_loop(0, steps, visit, 0)
    outs = (
        (sums.at[:, HALF:, STRIP:, :], give_low_ref),
        (sums.at[:, HALF:, :STRIP, :], give_up_ref),
        (sums.at[:, :HALF, STRIP:, :], keep_low_ref),
        (sums.at[:, :HALF, :STRIP, :], keep_up_ref),
    )
    started = [pltpu.make_async_copy(a, b, sems.at[n]) for n, (a, b) in enumerate(outs)]
    for copy in started:
        copy.start()
    lax.fori_loop(steps, groups, skip, 0)
    for copy in started:
        copy.wait()


def run_positions(scalars, probe, amps, tables, first, mine, other):
    from_strips = first is not None
    quarter = jax.ShapeDtypeStruct((3, HALF, STRIP, PATCH), jnp.float32)

    def kernel(*refs):
        if from_strips:
            positions_kernel(True, *refs)
        else:
            positions_kernel(False, *refs[:4], None, *refs[4:])

    pieces = (first, mine, other) if from_strips else (mine, other)
    return pl.pallas_call(
        kernel,
        out_shape=(quarter,) * 4 + (jax.ShapeDtypeStruct((3, PATCH, PATCH), jnp.float32),),
        in_specs=[ANY, VMEM] + [ANY] * (2 + len(pieces)),
        out_specs=(ANY,) * 4 + (VMEM,),
        scratch_shapes=[
            pltpu.VMEM((2, BLOCKS, BAND, PATCH), jnp.float32),
            pltpu.VMEM((3, BLOCKS, BAND, PATCH), jnp.float32),
            pltpu.VMEM(amps.shape, jnp.float32),
            pltpu.VMEM(tables.shape, tables.dtype),
            pltpu.SMEM(scalars.shape, jnp.int32),
            pltpu.SemaphoreType.DMA((2 * BLOCKS + 2,)),
            pltpu.SemaphoreType.DMA((amps.shape[0] // GROUP,)),
        ],
        compiler_params=pltpu.CompilerParams(vmem_limit_bytes=60 * 2**20),
        cost_estimate=pl.CostEstimate(
            flops=13 * 10**9, bytes_accessed=8 * 2**20, transcendentals=2**19
        ),
        name="positions",
    )(scalars, probe, amps, tables, *pieces)


def halved_over_cores(value):
    core = lax.axis_index("pos")
    lines = value.reshape(2, -1, PATCH)
    mine = lax.dynamic_index_in_dim(lines, core, 0, False)
    other = lax.dynamic_index_in_dim(lines, 1 - core, 0, False)
    return mine + swapped(other)


def joined_over_cores(part):
    first = lax.axis_index("pos") == 0
    other = swapped(part)
    low = jnp.where(first, part, other)
    high = jnp.where(first, other, part)
    return jnp.concatenate([low, high])


def summed_over(part, axis):
    count = lax.axis_size(axis)
    stride = 1
    while stride < count:
        fan = 4 if count % (stride * 4) == 0 else 2
        part = shifts_among(part, axis, stride, fan)
        stride *= fan
    return part


def after(value, other):
    return value + jnp.minimum(jnp.abs(other[0, 0]), 0.0)


def shifts_among(value, axis, stride, fan):
    count = lax.axis_size(axis)
    total = value
    for step in range(1, fan):
        route = []
        for i in range(count):
            place = i // stride % fan
            route.append((i, i + ((place + step) % fan - place) * stride))
        total = total + lax.ppermute(value, axis, route)
    return total


def in_blocks(value):
    lines = value.reshape(*value.shape[:2], HALF, PATCH)
    return lines.transpose(0, 2, 1, 3)


def on_device(object_field, probe_field, amplitudes, scan_rows, scan_cols, live_count):
    tables = dft_tables()
    core = lax.axis_index("pos")
    amps = amplitudes[0, 0]
    last = jnp.concatenate([live_count[0], core.astype(jnp.int32)[None]])
    lines = [scan_rows[0, 0], scan_cols[0, 0], last]
    scalars = jnp.stack([jnp.pad(line, (0, PATCH - line.shape[0])) for line in lines])
    scalars = jnp.pad(scalars, ((0, 8 - len(lines)), (0, 0)))
    probe_relax = amps.shape[0] * lax.axis_size(TILE) * lax.axis_size("pos") / 4.0
    own_half = lax.dynamic_slice_in_dim(object_field, core * (COLS // 2), COLS // 2, 2)
    halo = from_tile(own_half, 1)
    halo_other = swapped(halo)
    up, low, give_up, give_low, probe_sums = run_positions(
        scalars, probe_field, amps, tables, object_field, halo, halo_other
    )

    def next_probe(part, probe):
        for axis in TILE[1::-1]:
            part = summed_over(part, axis)
        total = joined_over_cores(part).reshape(3, PATCH, PATCH)
        return (total[:2] + probe_relax * probe) / (total[2] + probe_relax)[None]

    def updated(sums, field):
        return (sums[:2] + OBJECT_RELAX * field) / (sums[2] + OBJECT_RELAX)[None]

    part = summed_over(halved_over_cores(probe_sums), TILE[2])
    low = after(low + swapped(give_low), part)
    up = after(up + swapped(give_up), part)
    above = from_tile(low, -1)
    below = from_tile(up, 1)
    probe_field = next_probe(part, probe_field)
    own_half = updated(up + above, in_blocks(own_half))
    mine = jnp.concatenate([own_half, updated(low + below, in_blocks(halo))], axis=2)
    other = swapped(mine)
    up, low, give_up, give_low, probe_sums = run_positions(
        scalars, probe_field, amps, tables, None, mine, other
    )
    part = summed_over(halved_over_cores(probe_sums), TILE[2])
    low = after(low + swapped(give_low), part)
    up = up + swapped(give_up)
    above = from_tile(low, -1)
    probe_out = next_probe(part, probe_field)
    mine = updated(up + above, own_half).transpose(0, 2, 1, 3).reshape(2, STRIP, COLS // 2)
    other = swapped(mine)
    left = jnp.where(core == 0, mine, other)
    right = jnp.where(core == 0, other, mine)
    return jnp.concatenate([left, right], axis=2), probe_out


def torus_of(mesh):
    shape = (mesh.shape["tile"],)
    shape = (8, 4, 4) if shape == (128,) else (1, 1, *shape)
    return Mesh(mesh.devices.reshape(*shape, mesh.shape["pos"]), (*TILE, "pos"))


def solution(mesh):
    return jax.shard_map(
        on_device,
        mesh=torus_of(mesh),
        in_specs=(
            P(None, TILE, None),
            P(),
            P(TILE, "pos", None, None, None),
            P(TILE, "pos", None),
            P(TILE, "pos", None),
            P(TILE, "pos"),
        ),
        out_specs=(P(None, TILE, None), P()),
        check_vma=False,
    )
```

```python
import math

import jax
import jax.numpy as jnp
import numpy as np
from jax import lax
from jax.experimental import pallas as pl
from jax.experimental.pallas import tpu as pltpu
from jax.sharding import Mesh
from jax.sharding import PartitionSpec as P

PATCH = 128
STRIP = 128
COLS = 1024
BLOCKS = COLS // PATCH
HALF = BLOCKS // 2
BAND = 2 * STRIP
GROUP = 8
ITERS = 2
TILE = ("tile_0", "tile_1", "tile_2")
MODULUS_FLOOR = 0.2
OBJECT_RELAX = 1.0
ANY = pl.BlockSpec(memory_space=pl.ANY)
VMEM = pl.BlockSpec(memory_space=pltpu.VMEM)


def swapped(value):
    return lax.ppermute(value, "pos", [(0, 1), (1, 0)])


def from_tile(value, distance):
    count = lax.axis_size(TILE)
    return lax.ppermute(value, TILE, [((i + distance) % count, i) for i in range(count)])


def two_terms(value):
    high = value.astype(jnp.bfloat16)
    low = (value - high.astype(jnp.float32)).astype(jnp.bfloat16)
    return high, low


def dft_tables():
    counter = np.arange(PATCH)
    angle = (counter[:, None] * counter[None, :] % PATCH) * (2.0 * math.pi / PATCH)
    cosine = np.cos(angle) / math.sqrt(PATCH)
    sine = np.sin(angle) / math.sqrt(PATCH)
    tables = []
    for sign in (1.0, -1.0):
        for turn in (1.0, -1.0):
            cross = sign * turn * sine
            table = np.block([[cosine, -cross], [cross, cosine]]).astype(np.float32)
            high = table.astype(jnp.bfloat16)
            tables += [high, (table - high.astype(np.float32)).astype(jnp.bfloat16)]
    return jnp.asarray(np.stack(tables))


def times_right(real, imag, high_table, low_table):
    stacked = jnp.concatenate(
        [jnp.concatenate([r, i], axis=1) for r, i in zip(real, imag)], axis=0
    )
    high, low = two_terms(stacked)
    wide = jnp.concatenate([high, low, high], axis=1)
    table = jnp.concatenate([high_table, high_table, low_table], axis=0)
    out = jnp.dot(wide, table, preferred_element_type=jnp.float32)
    return (
        [out[k * PATCH : (k + 1) * PATCH, :PATCH] for k in range(len(real))],
        [out[k * PATCH : (k + 1) * PATCH, PATCH:] for k in range(len(real))],
    )


def times_left(real, imag, high_table, low_table):
    stacked = jnp.concatenate(
        [jnp.concatenate(real, axis=1), jnp.concatenate(imag, axis=1)], axis=0
    )
    high, low = two_terms(stacked)
    tall = jnp.concatenate([high, low, high], axis=0)
    table = jnp.concatenate([high_table, high_table, low_table], axis=1)
    out = jnp.dot(table, tall, preferred_element_type=jnp.float32)
    return (
        [out[:PATCH, k * PATCH : (k + 1) * PATCH] for k in range(len(real))],
        [out[PATCH:, k * PATCH : (k + 1) * PATCH] for k in range(len(real))],
    )


def column_place(col, own_first):
    block = col // PATCH
    near = block ^ own_first
    far = ((block + 1) % BLOCKS) ^ own_first
    return near, far, col % PATCH


def positions_kernel(
    from_strips,
    rows_hbm,
    cols_hbm,
    live_hbm,
    probe_ref,
    amps_hbm,
    tables_hbm,
    first_ref,
    mine_ref,
    other_ref,
    keep_up_ref,
    keep_low_ref,
    give_up_ref,
    give_low_ref,
    keep_probe_ref,
    give_probe_ref,
    probe_sums_ref,
    band,
    sums,
    amps_ref,
    tables,
    rows_ref,
    cols_ref,
    live_ref,
    sems,
    amp_sems,
):
    core = lax.axis_index("pos").astype(jnp.int32)
    here = lax.axis_index(TILE[2]).astype(jnp.int32)
    own_first = core * HALF

    def amp_copy(group):
        place = pl.ds(group * GROUP, GROUP)
        return pltpu.make_async_copy(amps_hbm.at[place], amps_ref.at[place], amp_sems.at[group])

    copies = [
        (tables_hbm, tables),
        (rows_hbm, rows_ref),
        (cols_hbm, cols_ref),
        (live_hbm, live_ref),
    ]
    if from_strips:
        for k in range(BLOCKS):
            start = pl.multiple_of((k ^ own_first) * PATCH, PATCH)
            copies.append((first_ref.at[:, :, pl.ds(start, PATCH)], band.at[:, k, :STRIP, :]))
            half = mine_ref if k < HALF else other_ref
            columns = pl.ds(k % HALF * PATCH, PATCH)
            copies.append((half.at[:, :, columns], band.at[:, k, STRIP:, :]))
    else:
        copies.append((mine_ref, band.at[:, :HALF]))
        copies.append((other_ref, band.at[:, HALF:]))
    started = [pltpu.make_async_copy(a, b, sems.at[n]) for n, (a, b) in enumerate(copies)]
    for copy in started:
        copy.start()
    amp_copy(0).start()
    sums[...] = jnp.zeros_like(sums)
    probe_sums_ref[...] = jnp.zeros_like(probe_sums_ref)
    for copy in started:
        copy.wait()
    live = live_ref[0, 0]
    lane = lax.broadcasted_iota(jnp.int32, (PATCH, PATCH), 1)

    steps = (live + GROUP - 1) // GROUP

    def visit(step, carry):
        amp_copy(step).wait()

        @pl.when(step + 1 < steps)
        def _():
            amp_copy(step + 1).start()

        slots = [step * GROUP + k for k in range(GROUP)]
        places = [column_place(cols_ref[0, 0, s], own_first) for s in slots]
        rows = [rows_ref[0, 0, s] for s in slots]
        patches = {}
        waves = {}

        def cut(pair):
            probe_real, probe_imag = probe_ref[0], probe_ref[1]
            real, imag = [], []
            for k in (2 * pair, 2 * pair + 1):
                near, far, shift = places[k]
                back = (PATCH - shift) % PATCH
                patch = []
                for plane in range(2):
                    a = band[plane, near, pl.ds(rows[k], PATCH), :]
                    b = band[plane, far, pl.ds(rows[k], PATCH), :]
                    patch.append(pltpu.roll(jnp.where(lane >= shift, a, b), back, 1))
                patches[k] = patch
                real.append(probe_real * patch[0] - probe_imag * patch[1])
                imag.append(probe_real * patch[1] + probe_imag * patch[0])
            waves[pair] = (real, imag)

        def rescale(pair):
            real, imag = waves[pair]
            for k in range(2):
                slot = slots[2 * pair + k]
                power = real[k] * real[k] + imag[k] * imag[k]
                ratio = jnp.where(slot < live, amps_ref[slot], 0.0) * lax.rsqrt(
                    jnp.maximum(power, MODULUS_FLOOR * MODULUS_FLOOR)
                )
                real[k] = real[k] * ratio
                imag[k] = imag[k] * ratio

        def right(pair, table):
            waves[pair] = times_right(*waves[pair], tables[table], tables[table + 1])

        def left(pair, table):
            waves[pair] = times_left(*waves[pair], tables[table], tables[table + 1])

        def collect(pair):
            probe_real, probe_imag = probe_ref[0], probe_ref[1]
            probe_power = probe_real * probe_real + probe_imag * probe_imag
            totals = [0.0, 0.0, 0.0]
            for back_real, back_imag, k in zip(*waves[pair], (2 * pair, 2 * pair + 1)):
                alive = slots[k] < live
                patch_real, patch_imag = patches[k]
                patch_power = patch_real * patch_real + patch_imag * patch_imag
                totals[0] += patch_real * back_real + patch_imag * back_imag
                totals[1] += patch_real * back_imag - patch_imag * back_real
                totals[2] += jnp.where(alive, patch_power, 0.0)
                near, far, shift = places[k]
                terms = (
                    probe_real * back_real + probe_imag * back_imag,
                    probe_real * back_imag - probe_imag * back_real,
                    jnp.where(alive, probe_power, 0.0),
                )
                inside = lane >= shift
                for plane in range(3):
                    turned = pltpu.roll(terms[plane], shift, 1)
                    sums[plane, near, pl.ds(rows[k], PATCH), :] += jnp.where(inside, turned, 0.0)
                    sums[plane, far, pl.ds(rows[k], PATCH), :] += jnp.where(inside, 0.0, turned)
            for plane in range(3):
                probe_sums_ref[pl.ds(plane * PATCH, PATCH), :] += totals[plane]

        stages = (
            cut,
            lambda pair: right(pair, 0),
            lambda pair: left(pair, 2),
            rescale,
            lambda pair: left(pair, 6),
            lambda pair: right(pair, 4),
            collect,
        )
        pairs = GROUP // 2
        for stage in stages:
            for pair in range(pairs):
                stage(pair)
        return carry

    lax.fori_loop(0, steps, visit, 0)
    outs = [
        (sums.at[:, HALF:, STRIP:, :], give_low_ref),
        (sums.at[:, HALF:, :STRIP, :], give_up_ref),
        (sums.at[:, :HALF, STRIP:, :], keep_low_ref),
        (sums.at[:, :HALF, :STRIP, :], keep_up_ref),
    ]
    count, height, _ = keep_probe_ref.shape
    for half, out in ((core, keep_probe_ref), (1 - core, give_probe_ref)):
        for k in range(count):
            start = (half * count + (here + k) % count) * height
            outs.append((probe_sums_ref.at[pl.ds(pl.multiple_of(start, 8), height)], out.at[k]))
    started = [pltpu.make_async_copy(a, b, sems.at[n]) for n, (a, b) in enumerate(outs)]
    for copy in started:
        copy.start()
    for copy in started:
        copy.wait()


def run_positions(scalars, probe, amps, tables, first, mine, other):
    from_strips = first is not None
    quarter = jax.ShapeDtypeStruct((3, HALF, STRIP, PATCH), jnp.float32)
    count = lax.axis_size(TILE[2])
    pieces_of = jax.ShapeDtypeStruct((count, 3 * PATCH // (2 * count), PATCH), jnp.float32)

    def kernel(*refs):
        if from_strips:
            positions_kernel(True, *refs)
        else:
            positions_kernel(False, *refs[:6], None, *refs[6:])

    pieces = (first, mine, other) if from_strips else (mine, other)
    return pl.pallas_call(
        kernel,
        out_shape=(quarter,) * 4 + (pieces_of,) * 2,
        in_specs=[ANY] * 3 + [VMEM] + [ANY] * (2 + len(pieces)),
        out_specs=(ANY,) * 6,
        scratch_shapes=[
            pltpu.VMEM((3 * PATCH, PATCH), jnp.float32),
            pltpu.VMEM((2, BLOCKS, BAND, PATCH), jnp.float32),
            pltpu.VMEM((3, BLOCKS, BAND, PATCH), jnp.float32),
            pltpu.VMEM(amps.shape, jnp.float32),
            pltpu.VMEM(tables.shape, tables.dtype),
            *(pltpu.SMEM(s.shape, jnp.int32) for s in scalars),
            pltpu.SemaphoreType.DMA((2 * BLOCKS + 4,)),
            pltpu.SemaphoreType.DMA((amps.shape[0] // GROUP,)),
        ],
        compiler_params=pltpu.CompilerParams(vmem_limit_bytes=60 * 2**20),
        cost_estimate=pl.CostEstimate(
            flops=13 * 10**9, bytes_accessed=8 * 2**20, transcendentals=2**19
        ),
        name="positions",
    )(*scalars, probe, amps, tables, *pieces)


def joined_over_cores(part):
    first = lax.axis_index("pos") == 0
    other = swapped(part)
    low = jnp.where(first, part, other)
    high = jnp.where(first, other, part)
    return jnp.concatenate([low, high])


def fans_of(count):
    fans = []
    stride = 1
    while stride < count:
        fans.append((stride, 4 if count % (stride * 4) == 0 else 2))
        stride *= fans[-1][1]
    return fans


def summed_over(part, axis):
    for stride, fan in fans_of(lax.axis_size(axis)):
        part = shifts_among(part, axis, stride, fan)
    return part


def scattered_over(pieces, axis):
    count = lax.axis_size(axis)
    arrived = []
    for step in range(1, count):
        route = [(i, (i + step) % count) for i in range(count)]
        arrived.append(lax.ppermute(pieces[step], axis, route))
    total = pieces[0]
    for piece in arrived:
        total = total + piece
    return total


def gathered_over(piece, axis):
    count = lax.axis_size(axis)
    here = lax.axis_index(axis)
    pieces = [piece]
    for step in range(1, count):
        pieces.append(lax.ppermute(piece, axis, [((i + step) % count, i) for i in range(count)]))
    rows = []
    for place in range(count):
        row = pieces[0]
        for step in range(1, count):
            row = jnp.where((place - here) % count == step, pieces[step], row)
        rows.append(row)
    return jnp.concatenate(rows)


def after(value, other):
    return value + jnp.minimum(jnp.abs(other[(0,) * other.ndim]), 0.0)


def shifts_among(value, axis, stride, fan):
    count = lax.axis_size(axis)
    total = value
    for step in range(1, fan):
        route = []
        for i in range(count):
            place = i // stride % fan
            route.append((i, i + ((place + step) % fan - place) * stride))
        total = total + lax.ppermute(value, axis, route)
    return total


def in_blocks(value):
    lines = value.reshape(*value.shape[:2], HALF, PATCH)
    return lines.transpose(0, 2, 1, 3)


def on_device(object_field, probe_field, amplitudes, scan_rows, scan_cols, live_count):
    tables = dft_tables()
    core = lax.axis_index("pos")
    amps = amplitudes[0, 0]
    scalars = (scan_rows, scan_cols, live_count)
    probe_relax = amps.shape[0] * lax.axis_size(TILE) * lax.axis_size("pos") / 4.0
    own_half = lax.dynamic_slice_in_dim(object_field, core * (COLS // 2), COLS // 2, 2)
    halo = from_tile(own_half, 1)
    halo_other = swapped(halo)
    up, low, give_up, give_low, keep_sums, give_sums = run_positions(
        scalars, probe_field, amps, tables, object_field, halo, halo_other
    )

    def next_probe(part, earlier, probe):
        part = gathered_over(part, TILE[2])
        if earlier is not None:
            part = after(part, earlier)
        total = joined_over_cores(part).reshape(3, PATCH, PATCH)
        return (total[:2] + probe_relax * probe) / (total[2] + probe_relax)[None]

    def updated(sums, field):
        return (sums[:2] + OBJECT_RELAX * field) / (sums[2] + OBJECT_RELAX)[None]

    part = scattered_over(keep_sums + swapped(give_sums), TILE[2])
    low = after(low + swapped(give_low), part)
    up = after(up + swapped(give_up), part)
    above = from_tile(low, -1)
    below = from_tile(up, 1)
    part = summed_over(summed_over(part, TILE[1]), TILE[0])
    up, low, above, below = lax.optimization_barrier((up, low, above, below))
    own_half = updated(up + above, in_blocks(own_half))
    mine = jnp.concatenate([own_half, updated(low + below, in_blocks(halo))], axis=2)
    other = swapped(mine)
    probe_field = next_probe(part, None, probe_field)
    up, low, give_up, give_low, keep_sums, give_sums = run_positions(
        scalars, probe_field, amps, tables, None, mine, other
    )
    part = scattered_over(keep_sums + swapped(give_sums), TILE[2])
    low = after(low + swapped(give_low), part)
    up = up + swapped(give_up)
    above = from_tile(low, -1)
    part = summed_over(summed_over(part, TILE[1]), TILE[0])
    up = after(up, part)
    mine = updated(up + above, own_half).transpose(0, 2, 1, 3).reshape(2, STRIP, COLS // 2)
    other = swapped(mine)
    left = jnp.where(core == 0, mine, other)
    right = jnp.where(core == 0, other, mine)
    object_out = jnp.concatenate([left, right], axis=2)
    probe_out = next_probe(part, object_out, probe_field)
    return object_out, probe_out


def torus_of(mesh):
    shape = (mesh.shape["tile"],)
    shape = (8, 4, 4) if shape == (128,) else (1, 1, *shape)
    return Mesh(mesh.devices.reshape(*shape, mesh.shape["pos"]), (*TILE, "pos"))


def solution(mesh):
    return jax.shard_map(
        on_device,
        mesh=torus_of(mesh),
        in_specs=(
            P(None, TILE, None),
            P(),
            P(TILE, "pos", None, None, None),
            P(TILE, "pos", None),
            P(TILE, "pos", None),
            P(TILE, "pos"),
        ),
        out_specs=(P(None, TILE, None), P()),
        check_vma=False,
    )
```

```python
import math

import jax
import jax.numpy as jnp
import numpy as np
from jax import lax
from jax.experimental import pallas as pl
from jax.experimental.pallas import tpu as pltpu
from jax.sharding import Mesh
from jax.sharding import PartitionSpec as P

PATCH = 128
STRIP = 128
COLS = 1024
BLOCKS = COLS // PATCH
HALF = BLOCKS // 2
BAND = 2 * STRIP
GROUP = 8
ITERS = 2
TILE = ("tile_0", "tile_1", "tile_2")
MODULUS_FLOOR = 0.2
OBJECT_RELAX = 1.0
ANY = pl.BlockSpec(memory_space=pl.ANY)
VMEM = pl.BlockSpec(memory_space=pltpu.VMEM)


def swapped(value):
    return lax.ppermute(value, "pos", [(0, 1), (1, 0)])


def from_tile(value, distance):
    count = lax.axis_size(TILE)
    return lax.ppermute(value, TILE, [((i + distance) % count, i) for i in range(count)])


def two_terms(value):
    high = value.astype(jnp.bfloat16)
    low = (value - high.astype(jnp.float32)).astype(jnp.bfloat16)
    return high, low


def dft_tables():
    counter = np.arange(PATCH)
    angle = (counter[:, None] * counter[None, :] % PATCH) * (2.0 * math.pi / PATCH)
    cosine = np.cos(angle) / math.sqrt(PATCH)
    sine = np.sin(angle) / math.sqrt(PATCH)
    tables = []
    for sign in (1.0, -1.0):
        for turn in (1.0, -1.0):
            cross = sign * turn * sine
            table = np.block([[cosine, -cross], [cross, cosine]]).astype(np.float32)
            high = table.astype(jnp.bfloat16)
            tables += [high, (table - high.astype(np.float32)).astype(jnp.bfloat16)]
    return jnp.asarray(np.stack(tables))


def times_right(real, imag, high_table, low_table):
    stacked = jnp.concatenate(
        [jnp.concatenate([r, i], axis=1) for r, i in zip(real, imag)], axis=0
    )
    high, low = two_terms(stacked)
    wide = jnp.concatenate([high, low, high], axis=1)
    table = jnp.concatenate([high_table, high_table, low_table], axis=0)
    out = jnp.dot(wide, table, preferred_element_type=jnp.float32)
    return (
        [out[k * PATCH : (k + 1) * PATCH, :PATCH] for k in range(len(real))],
        [out[k * PATCH : (k + 1) * PATCH, PATCH:] for k in range(len(real))],
    )


def times_left(real, imag, high_table, low_table):
    stacked = jnp.concatenate(
        [jnp.concatenate(real, axis=1), jnp.concatenate(imag, axis=1)], axis=0
    )
    high, low = two_terms(stacked)
    tall = jnp.concatenate([high, low, high], axis=0)
    table = jnp.concatenate([high_table, high_table, low_table], axis=1)
    out = jnp.dot(table, tall, preferred_element_type=jnp.float32)
    return (
        [out[:PATCH, k * PATCH : (k + 1) * PATCH] for k in range(len(real))],
        [out[PATCH:, k * PATCH : (k + 1) * PATCH] for k in range(len(real))],
    )


def column_place(col, own_first):
    block = col // PATCH
    near = block ^ own_first
    far = ((block + 1) % BLOCKS) ^ own_first
    return near, far, col % PATCH


def positions_kernel(
    from_strips,
    rows_hbm,
    cols_hbm,
    live_hbm,
    probe_ref,
    amps_hbm,
    tables_hbm,
    first_ref,
    mine_ref,
    other_ref,
    keep_up_ref,
    keep_low_ref,
    give_up_ref,
    give_low_ref,
    keep_probe_ref,
    give_probe_ref,
    probe_sums_ref,
    band,
    sums,
    amps_ref,
    tables,
    rows_ref,
    cols_ref,
    live_ref,
    sems,
    amp_sems,
):
    core = lax.axis_index("pos").astype(jnp.int32)
    here = lax.axis_index(TILE[2]).astype(jnp.int32)
    own_first = core * HALF

    def amp_copy(group):
        place = pl.ds(group * GROUP, GROUP)
        return pltpu.make_async_copy(amps_hbm.at[place], amps_ref.at[place], amp_sems.at[group])

    copies = [
        (tables_hbm, tables),
        (rows_hbm, rows_ref),
        (cols_hbm, cols_ref),
        (live_hbm, live_ref),
    ]
    if from_strips:
        for k in range(BLOCKS):
            start = pl.multiple_of((k ^ own_first) * PATCH, PATCH)
            copies.append((first_ref.at[:, :, pl.ds(start, PATCH)], band.at[:, k, :STRIP, :]))
            half = mine_ref if k < HALF else other_ref
            columns = pl.ds(k % HALF * PATCH, PATCH)
            copies.append((half.at[:, :, columns], band.at[:, k, STRIP:, :]))
    else:
        copies.append((mine_ref, band.at[:, :HALF]))
        copies.append((other_ref, band.at[:, HALF:]))
    started = [pltpu.make_async_copy(a, b, sems.at[n]) for n, (a, b) in enumerate(copies)]
    for copy in started:
        copy.start()
    amp_copy(0).start()
    sums[...] = jnp.zeros_like(sums)
    probe_sums_ref[...] = jnp.zeros_like(probe_sums_ref)
    for copy in started:
        copy.wait()
    live = live_ref[0, 0]
    lane = lax.broadcasted_iota(jnp.int32, (PATCH, PATCH), 1)

    steps = (live + GROUP - 1) // GROUP

    def visit(step, carry):
        amp_copy(step).wait()

        @pl.when(step + 1 < steps)
        def _():
            amp_copy(step + 1).start()

        slots = [step * GROUP + k for k in range(GROUP)]
        places = [column_place(cols_ref[0, 0, s], own_first) for s in slots]
        rows = [rows_ref[0, 0, s] for s in slots]
        patches = {}
        waves = {}

        def cut(pair):
            probe_real, probe_imag = probe_ref[0], probe_ref[1]
            real, imag = [], []
            for k in (2 * pair, 2 * pair + 1):
                near, far, shift = places[k]
                back = (PATCH - shift) % PATCH
                patch = []
                for plane in range(2):
                    a = band[plane, near, pl.ds(rows[k], PATCH), :]
                    b = band[plane, far, pl.ds(rows[k], PATCH), :]
                    patch.append(pltpu.roll(jnp.where(lane >= shift, a, b), back, 1))
                patches[k] = patch
                real.append(probe_real * patch[0] - probe_imag * patch[1])
                imag.append(probe_real * patch[1] + probe_imag * patch[0])
            waves[pair] = (real, imag)

        def rescale(pair):
            real, imag = waves[pair]
            for k in range(2):
                slot = slots[2 * pair + k]
                power = real[k] * real[k] + imag[k] * imag[k]
                ratio = jnp.where(slot < live, amps_ref[slot], 0.0) * lax.rsqrt(
                    jnp.maximum(power, MODULUS_FLOOR * MODULUS_FLOOR)
                )
                real[k] = real[k] * ratio
                imag[k] = imag[k] * ratio

        def right(pair, table):
            waves[pair] = times_right(*waves[pair], tables[table], tables[table + 1])

        def left(pair, table):
            waves[pair] = times_left(*waves[pair], tables[table], tables[table + 1])

        def collect(pair):
            probe_real, probe_imag = probe_ref[0], probe_ref[1]
            probe_power = probe_real * probe_real + probe_imag * probe_imag
            totals = [0.0, 0.0, 0.0]
            for back_real, back_imag, k in zip(*waves[pair], (2 * pair, 2 * pair + 1)):
                alive = slots[k] < live
                patch_real, patch_imag = patches[k]
                patch_power = patch_real * patch_real + patch_imag * patch_imag
                totals[0] += patch_real * back_real + patch_imag * back_imag
                totals[1] += patch_real * back_imag - patch_imag * back_real
                totals[2] += jnp.where(alive, patch_power, 0.0)
                near, far, shift = places[k]
                terms = (
                    probe_real * back_real + probe_imag * back_imag,
                    probe_real * back_imag - probe_imag * back_real,
                    jnp.where(alive, probe_power, 0.0),
                )
                inside = lane >= shift
                for plane in range(3):
                    turned = pltpu.roll(terms[plane], shift, 1)
                    sums[plane, near, pl.ds(rows[k], PATCH), :] += jnp.where(inside, turned, 0.0)
                    sums[plane, far, pl.ds(rows[k], PATCH), :] += jnp.where(inside, 0.0, turned)
            for plane in range(3):
                probe_sums_ref[pl.ds(plane * PATCH, PATCH), :] += totals[plane]

        stages = (
            cut,
            lambda pair: right(pair, 0),
            lambda pair: left(pair, 2),
            rescale,
            lambda pair: left(pair, 6),
            lambda pair: right(pair, 4),
            collect,
        )
        pairs = GROUP // 2
        for stage in stages:
            for pair in range(pairs):
                stage(pair)
        return carry

    lax.fori_loop(0, steps, visit, 0)
    outs = [
        (sums.at[:, HALF:, STRIP:, :], give_low_ref),
        (sums.at[:, HALF:, :STRIP, :], give_up_ref),
        (sums.at[:, :HALF, STRIP:, :], keep_low_ref),
        (sums.at[:, :HALF, :STRIP, :], keep_up_ref),
    ]
    count, height, _ = keep_probe_ref.shape
    for half, out in ((core, keep_probe_ref), (1 - core, give_probe_ref)):
        for k in range(count):
            start = (half * count + (here + k) % count) * height
            outs.append((probe_sums_ref.at[pl.ds(pl.multiple_of(start, 8), height)], out.at[k]))
    started = [pltpu.make_async_copy(a, b, sems.at[n]) for n, (a, b) in enumerate(outs)]
    for copy in started:
        copy.start()
    for copy in started:
        copy.wait()


def run_positions(scalars, probe, amps, tables, first, mine, other):
    from_strips = first is not None
    quarter = jax.ShapeDtypeStruct((3, HALF, STRIP, PATCH), jnp.float32)
    count = lax.axis_size(TILE[2])
    pieces_of = jax.ShapeDtypeStruct((count, 3 * PATCH // (2 * count), PATCH), jnp.float32)

    def kernel(*refs):
        if from_strips:
            positions_kernel(True, *refs)
        else:
            positions_kernel(False, *refs[:6], None, *refs[6:])

    pieces = (first, mine, other) if from_strips else (mine, other)
    return pl.pallas_call(
        kernel,
        out_shape=(quarter,) * 4 + (pieces_of,) * 2,
        in_specs=[ANY] * 3 + [VMEM] + [ANY] * (2 + len(pieces)),
        out_specs=(ANY,) * 6,
        scratch_shapes=[
            pltpu.VMEM((3 * PATCH, PATCH), jnp.float32),
            pltpu.VMEM((2, BLOCKS, BAND, PATCH), jnp.float32),
            pltpu.VMEM((3, BLOCKS, BAND, PATCH), jnp.float32),
            pltpu.VMEM(amps.shape, jnp.float32),
            pltpu.VMEM(tables.shape, tables.dtype),
            *(pltpu.SMEM(s.shape, jnp.int32) for s in scalars),
            pltpu.SemaphoreType.DMA((2 * BLOCKS + 4,)),
            pltpu.SemaphoreType.DMA((amps.shape[0] // GROUP,)),
        ],
        compiler_params=pltpu.CompilerParams(vmem_limit_bytes=60 * 2**20),
        cost_estimate=pl.CostEstimate(
            flops=13 * 10**9, bytes_accessed=8 * 2**20, transcendentals=2**19
        ),
        name="positions",
    )(*scalars, probe, amps, tables, *pieces)


def joined_over_cores(part):
    first = lax.axis_index("pos") == 0
    other = swapped(part)
    low = jnp.where(first, part, other)
    high = jnp.where(first, other, part)
    return jnp.concatenate([low, high])


def fans_of(count):
    fans = []
    stride = 1
    while stride < count:
        fans.append((stride, 4 if count % (stride * 4) == 0 else 2))
        stride *= fans[-1][1]
    return fans


def summed_over(part, axis):
    for stride, fan in fans_of(lax.axis_size(axis)):
        part = shifts_among(part, axis, stride, fan)
    return part


def scattered_over(pieces, axis):
    count = lax.axis_size(axis)
    arrived = []
    for step in range(1, count):
        route = [(i, (i + step) % count) for i in range(count)]
        arrived.append(lax.ppermute(pieces[step], axis, route))
    total = pieces[0]
    for piece in arrived:
        total = total + piece
    return total


def gathered_over(piece, axis):
    count = lax.axis_size(axis)
    here = lax.axis_index(axis)
    pieces = [piece]
    for step in range(1, count):
        pieces.append(lax.ppermute(piece, axis, [((i + step) % count, i) for i in range(count)]))
    rows = []
    for place in range(count):
        row = pieces[0]
        for step in range(1, count):
            row = jnp.where((place - here) % count == step, pieces[step], row)
        rows.append(row)
    return jnp.concatenate(rows)


def after(value, other):
    return value + jnp.minimum(jnp.abs(other[(0,) * other.ndim]), 0.0)


def shifts_among(value, axis, stride, fan):
    count = lax.axis_size(axis)
    total = value
    for step in range(1, fan):
        route = []
        for i in range(count):
            place = i // stride % fan
            route.append((i, i + ((place + step) % fan - place) * stride))
        total = total + lax.ppermute(value, axis, route)
    return total


def in_blocks(value):
    lines = value.reshape(*value.shape[:2], HALF, PATCH)
    return lines.transpose(0, 2, 1, 3)


def on_device(object_field, probe_field, amplitudes, scan_rows, scan_cols, live_count):
    tables = dft_tables()
    core = lax.axis_index("pos")
    amps = amplitudes[0, 0]
    scalars = (scan_rows, scan_cols, live_count)
    probe_relax = amps.shape[0] * lax.axis_size(TILE) * lax.axis_size("pos") / 4.0
    own_half = lax.dynamic_slice_in_dim(object_field, core * (COLS // 2), COLS // 2, 2)
    halo = from_tile(own_half, 1)
    halo_other = swapped(halo)
    up, low, give_up, give_low, keep_sums, give_sums = run_positions(
        scalars, probe_field, amps, tables, object_field, halo, halo_other
    )

    def next_probe(part, earlier, probe):
        part = gathered_over(part, TILE[2])
        if earlier is not None:
            part = after(part, earlier)
        total = joined_over_cores(part).reshape(3, PATCH, PATCH)
        return (total[:2] + probe_relax * probe) / (total[2] + probe_relax)[None]

    def updated(sums, field):
        return (sums[:2] + OBJECT_RELAX * field) / (sums[2] + OBJECT_RELAX)[None]

    part = scattered_over(keep_sums + swapped(give_sums), TILE[2])
    low = after(low + swapped(give_low), part)
    up = after(up + swapped(give_up), part)
    above = from_tile(low, -1)
    below = from_tile(up, 1)
    part = summed_over(summed_over(part, TILE[0]), TILE[1])
    up, low, above, below = lax.optimization_barrier((up, low, above, below))
    own_half = updated(up + above, in_blocks(own_half))
    mine = jnp.concatenate([own_half, updated(low + below, in_blocks(halo))], axis=2)
    other = swapped(mine)
    probe_field = next_probe(part, None, probe_field)
    up, low, give_up, give_low, keep_sums, give_sums = run_positions(
        scalars, probe_field, amps, tables, None, mine, other
    )
    part = scattered_over(keep_sums + swapped(give_sums), TILE[2])
    low = after(low + swapped(give_low), part)
    up = up + swapped(give_up)
    above = from_tile(low, -1)
    part = summed_over(summed_over(part, TILE[0]), TILE[1])
    up = after(up, part)
    mine = updated(up + above, own_half).transpose(0, 2, 1, 3).reshape(2, STRIP, COLS // 2)
    other = swapped(mine)
    left = jnp.where(core == 0, mine, other)
    right = jnp.where(core == 0, other, mine)
    object_out = jnp.concatenate([left, right], axis=2)
    probe_out = next_probe(part, object_out, probe_field)
    return object_out, probe_out


def torus_of(mesh):
    shape = (mesh.shape["tile"],)
    shape = (8, 4, 4) if shape == (128,) else (1, 1, *shape)
    return Mesh(mesh.devices.reshape(*shape, mesh.shape["pos"]), (*TILE, "pos"))


def solution(mesh):
    return jax.shard_map(
        on_device,
        mesh=torus_of(mesh),
        in_specs=(
            P(None, TILE, None),
            P(),
            P(TILE, "pos", None, None, None),
            P(TILE, "pos", None),
            P(TILE, "pos", None),
            P(TILE, "pos"),
        ),
        out_specs=(P(None, TILE, None), P()),
        check_vma=False,
    )
```

```python
import math

import jax
import jax.numpy as jnp
import numpy as np
from jax import lax
from jax.experimental import pallas as pl
from jax.experimental.pallas import tpu as pltpu
from jax.sharding import Mesh
from jax.sharding import PartitionSpec as P

PATCH = 128
STRIP = 128
COLS = 1024
BLOCKS = COLS // PATCH
HALF = BLOCKS // 2
BAND = 2 * STRIP
GROUP = 8
ITERS = 2
TILE = ("tile_0", "tile_1", "tile_2")
MODULUS_FLOOR = 0.2
OBJECT_RELAX = 1.0
ANY = pl.BlockSpec(memory_space=pl.ANY)
VMEM = pl.BlockSpec(memory_space=pltpu.VMEM)


def swapped(value):
    return lax.ppermute(value, "pos", [(0, 1), (1, 0)])


def from_tile(value, distance):
    count = lax.axis_size(TILE)
    return lax.ppermute(value, TILE, [((i + distance) % count, i) for i in range(count)])


def two_terms(value):
    high = value.astype(jnp.bfloat16)
    low = (value - high.astype(jnp.float32)).astype(jnp.bfloat16)
    return high, low


def dft_tables():
    counter = np.arange(PATCH)
    angle = (counter[:, None] * counter[None, :] % PATCH) * (2.0 * math.pi / PATCH)
    cosine = np.cos(angle) / math.sqrt(PATCH)
    sine = np.sin(angle) / math.sqrt(PATCH)
    tables = []
    for sign in (1.0, -1.0):
        for turn in (1.0, -1.0):
            cross = sign * turn * sine
            table = np.block([[cosine, -cross], [cross, cosine]]).astype(np.float32)
            high = table.astype(jnp.bfloat16)
            tables += [high, (table - high.astype(np.float32)).astype(jnp.bfloat16)]
    return jnp.asarray(np.stack(tables))


def times_right(real, imag, high_table, low_table):
    stacked = jnp.concatenate(
        [jnp.concatenate([r, i], axis=1) for r, i in zip(real, imag)], axis=0
    )
    high, low = two_terms(stacked)
    wide = jnp.concatenate([high, low, high], axis=1)
    table = jnp.concatenate([high_table, high_table, low_table], axis=0)
    out = jnp.dot(wide, table, preferred_element_type=jnp.float32)
    return (
        [out[k * PATCH : (k + 1) * PATCH, :PATCH] for k in range(len(real))],
        [out[k * PATCH : (k + 1) * PATCH, PATCH:] for k in range(len(real))],
    )


def times_left(real, imag, high_table, low_table):
    stacked = jnp.concatenate(
        [jnp.concatenate(real, axis=1), jnp.concatenate(imag, axis=1)], axis=0
    )
    high, low = two_terms(stacked)
    tall = jnp.concatenate([high, low, high], axis=0)
    table = jnp.concatenate([high_table, high_table, low_table], axis=1)
    out = jnp.dot(table, tall, preferred_element_type=jnp.float32)
    return (
        [out[:PATCH, k * PATCH : (k + 1) * PATCH] for k in range(len(real))],
        [out[PATCH:, k * PATCH : (k + 1) * PATCH] for k in range(len(real))],
    )


def column_place(col, own_first):
    block = col // PATCH
    near = block ^ own_first
    far = ((block + 1) % BLOCKS) ^ own_first
    return near, far, col % PATCH


def positions_kernel(
    from_strips,
    rows_hbm,
    cols_hbm,
    live_hbm,
    probe_ref,
    amps_hbm,
    tables_hbm,
    first_ref,
    mine_ref,
    other_ref,
    keep_up_ref,
    keep_low_ref,
    give_up_ref,
    give_low_ref,
    keep_probe_ref,
    give_probe_ref,
    probe_sums_ref,
    band,
    sums,
    amps_ref,
    tables,
    rows_ref,
    cols_ref,
    live_ref,
    sems,
    amp_sems,
):
    core = lax.axis_index("pos").astype(jnp.int32)
    here = lax.axis_index(TILE[2]).astype(jnp.int32)
    own_first = core * HALF

    def amp_copy(group):
        place = pl.ds(group * GROUP, GROUP)
        return pltpu.make_async_copy(amps_hbm.at[place], amps_ref.at[place], amp_sems.at[group])

    copies = [
        (tables_hbm, tables),
        (rows_hbm, rows_ref),
        (cols_hbm, cols_ref),
        (live_hbm, live_ref),
    ]
    if from_strips:
        for k in range(BLOCKS):
            start = pl.multiple_of((k ^ own_first) * PATCH, PATCH)
            copies.append((first_ref.at[:, :, pl.ds(start, PATCH)], band.at[:, k, :STRIP, :]))
            half = mine_ref if k < HALF else other_ref
            columns = pl.ds(k % HALF * PATCH, PATCH)
            copies.append((half.at[:, :, columns], band.at[:, k, STRIP:, :]))
    else:
        copies.append((mine_ref, band.at[:, :HALF]))
        copies.append((other_ref, band.at[:, HALF:]))
    started = [pltpu.make_async_copy(a, b, sems.at[n]) for n, (a, b) in enumerate(copies)]
    for copy in started:
        copy.start()
    amp_copy(0).start()
    sums[...] = jnp.zeros_like(sums)
    probe_sums_ref[...] = jnp.zeros_like(probe_sums_ref)
    for copy in started:
        copy.wait()
    live = live_ref[0, 0]
    lane = lax.broadcasted_iota(jnp.int32, (PATCH, PATCH), 1)

    steps = (live + GROUP - 1) // GROUP

    def visit(step, carry):
        amp_copy(step).wait()

        @pl.when(step + 1 < steps)
        def _():
            amp_copy(step + 1).start()

        slots = [step * GROUP + k for k in range(GROUP)]
        places = [column_place(cols_ref[0, 0, s], own_first) for s in slots]
        rows = [rows_ref[0, 0, s] for s in slots]
        patches = {}
        waves = {}

        def cut(pair):
            probe_real, probe_imag = probe_ref[0], probe_ref[1]
            real, imag = [], []
            for k in (2 * pair, 2 * pair + 1):
                near, far, shift = places[k]
                back = (PATCH - shift) % PATCH
                patch = []
                for plane in range(2):
                    a = band[plane, near, pl.ds(rows[k], PATCH), :]
                    b = band[plane, far, pl.ds(rows[k], PATCH), :]
                    patch.append(pltpu.roll(jnp.where(lane >= shift, a, b), back, 1))
                patches[k] = patch
                real.append(probe_real * patch[0] - probe_imag * patch[1])
                imag.append(probe_real * patch[1] + probe_imag * patch[0])
            waves[pair] = (real, imag)

        def rescale(pair):
            real, imag = waves[pair]
            for k in range(2):
                slot = slots[2 * pair + k]
                power = real[k] * real[k] + imag[k] * imag[k]
                ratio = jnp.where(slot < live, amps_ref[slot], 0.0) * lax.rsqrt(
                    jnp.maximum(power, MODULUS_FLOOR * MODULUS_FLOOR)
                )
                real[k] = real[k] * ratio
                imag[k] = imag[k] * ratio

        def right(pair, table):
            waves[pair] = times_right(*waves[pair], tables[table], tables[table + 1])

        def left(pair, table):
            waves[pair] = times_left(*waves[pair], tables[table], tables[table + 1])

        def collect(pair):
            probe_real, probe_imag = probe_ref[0], probe_ref[1]
            probe_power = probe_real * probe_real + probe_imag * probe_imag
            totals = [0.0, 0.0, 0.0]
            for back_real, back_imag, k in zip(*waves[pair], (2 * pair, 2 * pair + 1)):
                alive = slots[k] < live
                patch_real, patch_imag = patches[k]
                patch_power = patch_real * patch_real + patch_imag * patch_imag
                totals[0] += patch_real * back_real + patch_imag * back_imag
                totals[1] += patch_real * back_imag - patch_imag * back_real
                totals[2] += jnp.where(alive, patch_power, 0.0)
                near, far, shift = places[k]
                terms = (
                    probe_real * back_real + probe_imag * back_imag,
                    probe_real * back_imag - probe_imag * back_real,
                    jnp.where(alive, probe_power, 0.0),
                )
                inside = lane >= shift
                for plane in range(3):
                    turned = pltpu.roll(terms[plane], shift, 1)
                    sums[plane, near, pl.ds(rows[k], PATCH), :] += jnp.where(inside, turned, 0.0)
                    sums[plane, far, pl.ds(rows[k], PATCH), :] += jnp.where(inside, 0.0, turned)
            for plane in range(3):
                probe_sums_ref[pl.ds(plane * PATCH, PATCH), :] += totals[plane]

        stages = (
            cut,
            lambda pair: right(pair, 0),
            lambda pair: left(pair, 2),
            rescale,
            lambda pair: left(pair, 6),
            lambda pair: right(pair, 4),
            collect,
        )
        pairs = GROUP // 2
        for stage in stages:
            for pair in range(pairs):
                stage(pair)
        return carry

    lax.fori_loop(0, steps, visit, 0)
    outs = [
        (sums.at[:, HALF:, STRIP:, :], give_low_ref),
        (sums.at[:, HALF:, :STRIP, :], give_up_ref),
        (sums.at[:, :HALF, STRIP:, :], keep_low_ref),
        (sums.at[:, :HALF, :STRIP, :], keep_up_ref),
    ]
    count, height, _ = keep_probe_ref.shape
    for half, out in ((core, keep_probe_ref), (1 - core, give_probe_ref)):
        for k in range(count):
            start = (half * count + (here + k) % count) * height
            outs.append((probe_sums_ref.at[pl.ds(pl.multiple_of(start, 8), height)], out.at[k]))
    started = [pltpu.make_async_copy(a, b, sems.at[n]) for n, (a, b) in enumerate(outs)]
    for copy in started:
        copy.start()
    for copy in started:
        copy.wait()


def run_positions(scalars, probe, amps, tables, first, mine, other):
    from_strips = first is not None
    quarter = jax.ShapeDtypeStruct((3, HALF, STRIP, PATCH), jnp.float32)
    count = lax.axis_size(TILE[2])
    pieces_of = jax.ShapeDtypeStruct((count, 3 * PATCH // (2 * count), PATCH), jnp.float32)

    def kernel(*refs):
        if from_strips:
            positions_kernel(True, *refs)
        else:
            positions_kernel(False, *refs[:6], None, *refs[6:])

    pieces = (first, mine, other) if from_strips else (mine, other)
    return pl.pallas_call(
        kernel,
        out_shape=(quarter,) * 4 + (pieces_of,) * 2,
        in_specs=[ANY] * 3 + [VMEM] + [ANY] * (2 + len(pieces)),
        out_specs=(ANY,) * 6,
        scratch_shapes=[
            pltpu.VMEM((3 * PATCH, PATCH), jnp.float32),
            pltpu.VMEM((2, BLOCKS, BAND, PATCH), jnp.float32),
            pltpu.VMEM((3, BLOCKS, BAND, PATCH), jnp.float32),
            pltpu.VMEM(amps.shape, jnp.float32),
            pltpu.VMEM(tables.shape, tables.dtype),
            *(pltpu.SMEM(s.shape, jnp.int32) for s in scalars),
            pltpu.SemaphoreType.DMA((2 * BLOCKS + 4,)),
            pltpu.SemaphoreType.DMA((amps.shape[0] // GROUP,)),
        ],
        compiler_params=pltpu.CompilerParams(vmem_limit_bytes=60 * 2**20),
        cost_estimate=pl.CostEstimate(
            flops=13 * 10**9, bytes_accessed=8 * 2**20, transcendentals=2**19
        ),
        name="positions",
    )(*scalars, probe, amps, tables, *pieces)


def joined_over_cores(part):
    first = lax.axis_index("pos") == 0
    other = swapped(part)
    low = jnp.where(first, part, other)
    high = jnp.where(first, other, part)
    return jnp.concatenate([low, high])


def fans_of(count):
    fans = []
    stride = 1
    while stride < count:
        fans.append((stride, 4 if count % (stride * 4) == 0 else 2))
        stride *= fans[-1][1]
    return fans


def summed_over(part, axis):
    for stride, fan in fans_of(lax.axis_size(axis)):
        part = shifts_among(part, axis, stride, fan)
    return part


def moved_along(value, shift):
    depth, wide, high = (lax.axis_size(axis) for axis in TILE)
    route = []
    for place in range(depth * wide * high):
        line = place % (wide * high)
        step = shift if line == 0 else -shift
        route.append((place, (place // (wide * high) + step) % depth * wide * high + line))
    return lax.ppermute(value, TILE, route)


def summed_one_way(part):
    count = lax.axis_size(TILE[0])
    stride = 1
    while stride < count:
        arrived = part
        hops = 2 if stride > 2 else 1
        for _ in range(hops):
            arrived = moved_along(arrived, stride // hops)
        part = part + arrived
        stride *= 2
    return part


def scattered_over(pieces, axis):
    count = lax.axis_size(axis)
    arrived = []
    for step in range(1, count):
        route = [(i, (i + step) % count) for i in range(count)]
        arrived.append(lax.ppermute(pieces[step], axis, route))
    total = pieces[0]
    for piece in arrived:
        total = total + piece
    return total


def gathered_over(piece, axis):
    count = lax.axis_size(axis)
    here = lax.axis_index(axis)
    pieces = [piece]
    for step in range(1, count):
        pieces.append(lax.ppermute(piece, axis, [((i + step) % count, i) for i in range(count)]))
    rows = []
    for place in range(count):
        row = pieces[0]
        for step in range(1, count):
            row = jnp.where((place - here) % count == step, pieces[step], row)
        rows.append(row)
    return jnp.concatenate(rows)


def after(value, other):
    return value + jnp.minimum(jnp.abs(other[(0,) * other.ndim]), 0.0)


def shifts_among(value, axis, stride, fan):
    count = lax.axis_size(axis)
    total = value
    for step in range(1, fan):
        route = []
        for i in range(count):
            place = i // stride % fan
            route.append((i, i + ((place + step) % fan - place) * stride))
        total = total + lax.ppermute(value, axis, route)
    return total


def in_blocks(value):
    lines = value.reshape(*value.shape[:2], HALF, PATCH)
    return lines.transpose(0, 2, 1, 3)


def on_device(object_field, probe_field, amplitudes, scan_rows, scan_cols, live_count):
    tables = dft_tables()
    core = lax.axis_index("pos")
    amps = amplitudes[0, 0]
    scalars = (scan_rows, scan_cols, live_count)
    probe_relax = amps.shape[0] * lax.axis_size(TILE) * lax.axis_size("pos") / 4.0
    own_half = lax.dynamic_slice_in_dim(object_field, core * (COLS // 2), COLS // 2, 2)
    halo = from_tile(own_half, 1)
    halo_other = swapped(halo)
    up, low, give_up, give_low, keep_sums, give_sums = run_positions(
        scalars, probe_field, amps, tables, object_field, halo, halo_other
    )

    def next_probe(part, earlier, probe):
        part = gathered_over(part, TILE[2])
        if earlier is not None:
            part = after(part, earlier)
        total = joined_over_cores(part).reshape(3, PATCH, PATCH)
        return (total[:2] + probe_relax * probe) / (total[2] + probe_relax)[None]

    def updated(sums, field):
        return (sums[:2] + OBJECT_RELAX * field) / (sums[2] + OBJECT_RELAX)[None]

    part = scattered_over(keep_sums + swapped(give_sums), TILE[2])
    low = after(low + swapped(give_low), part)
    up = after(up + swapped(give_up), part)
    above = from_tile(low, -1)
    below = from_tile(up, 1)
    part = summed_over(summed_one_way(part), TILE[1])
    up, low, above, below = lax.optimization_barrier((up, low, above, below))
    own_half = updated(up + above, in_blocks(own_half))
    mine = jnp.concatenate([own_half, updated(low + below, in_blocks(halo))], axis=2)
    other = swapped(mine)
    probe_field = next_probe(part, None, probe_field)
    up, low, give_up, give_low, keep_sums, give_sums = run_positions(
        scalars, probe_field, amps, tables, None, mine, other
    )
    part = scattered_over(keep_sums + swapped(give_sums), TILE[2])
    low = after(low + swapped(give_low), part)
    up = up + swapped(give_up)
    above = from_tile(low, -1)
    part = summed_over(summed_one_way(part), TILE[1])
    up = after(up, part)
    mine = updated(up + above, own_half).transpose(0, 2, 1, 3).reshape(2, STRIP, COLS // 2)
    other = swapped(mine)
    left = jnp.where(core == 0, mine, other)
    right = jnp.where(core == 0, other, mine)
    object_out = jnp.concatenate([left, right], axis=2)
    probe_out = next_probe(part, object_out, probe_field)
    return object_out, probe_out


def torus_of(mesh):
    shape = (mesh.shape["tile"],)
    shape = (8, 4, 4) if shape == (128,) else (1, 1, *shape)
    return Mesh(mesh.devices.reshape(*shape, mesh.shape["pos"]), (*TILE, "pos"))


def solution(mesh):
    return jax.shard_map(
        on_device,
        mesh=torus_of(mesh),
        in_specs=(
            P(None, TILE, None),
            P(),
            P(TILE, "pos", None, None, None),
            P(TILE, "pos", None),
            P(TILE, "pos", None),
            P(TILE, "pos"),
        ),
        out_specs=(P(None, TILE, None), P()),
        check_vma=False,
    )
```

```python
import math

import jax
import jax.numpy as jnp
import numpy as np
from jax import lax
from jax.experimental import pallas as pl
from jax.experimental.pallas import tpu as pltpu
from jax.sharding import Mesh
from jax.sharding import PartitionSpec as P

PATCH = 128
STRIP = 128
COLS = 1024
BLOCKS = COLS // PATCH
HALF = BLOCKS // 2
BAND = 2 * STRIP
GROUP = 8
ITERS = 2
TILE = ("tile_0", "tile_1", "tile_2")
MODULUS_FLOOR = 0.2
OBJECT_RELAX = 1.0
ANY = pl.BlockSpec(memory_space=pl.ANY)
VMEM = pl.BlockSpec(memory_space=pltpu.VMEM)


def swapped(value):
    return lax.ppermute(value, "pos", [(0, 1), (1, 0)])


def from_tile(value, distance):
    count = lax.axis_size(TILE)
    return lax.ppermute(value, TILE, [((i + distance) % count, i) for i in range(count)])


def two_terms(value):
    high = value.astype(jnp.bfloat16)
    low = (value - high.astype(jnp.float32)).astype(jnp.bfloat16)
    return high, low


def dft_tables():
    counter = np.arange(PATCH)
    angle = (counter[:, None] * counter[None, :] % PATCH) * (2.0 * math.pi / PATCH)
    cosine = np.cos(angle) / math.sqrt(PATCH)
    sine = np.sin(angle) / math.sqrt(PATCH)
    tables = []
    for sign in (1.0, -1.0):
        for turn in (1.0, -1.0):
            cross = sign * turn * sine
            table = np.block([[cosine, -cross], [cross, cosine]]).astype(np.float32)
            high = table.astype(jnp.bfloat16)
            tables += [high, (table - high.astype(np.float32)).astype(jnp.bfloat16)]
    return jnp.asarray(np.stack(tables))


def times_right(real, imag, high_table, low_table):
    stacked = jnp.concatenate(
        [jnp.concatenate([r, i], axis=1) for r, i in zip(real, imag)], axis=0
    )
    high, low = two_terms(stacked)
    wide = jnp.concatenate([high, low, high], axis=1)
    table = jnp.concatenate([high_table, high_table, low_table], axis=0)
    out = jnp.dot(wide, table, preferred_element_type=jnp.float32)
    return (
        [out[k * PATCH : (k + 1) * PATCH, :PATCH] for k in range(len(real))],
        [out[k * PATCH : (k + 1) * PATCH, PATCH:] for k in range(len(real))],
    )


def times_left(real, imag, high_table, low_table):
    stacked = jnp.concatenate(
        [jnp.concatenate(real, axis=1), jnp.concatenate(imag, axis=1)], axis=0
    )
    high, low = two_terms(stacked)
    tall = jnp.concatenate([high, low, high], axis=0)
    table = jnp.concatenate([high_table, high_table, low_table], axis=1)
    out = jnp.dot(table, tall, preferred_element_type=jnp.float32)
    return (
        [out[:PATCH, k * PATCH : (k + 1) * PATCH] for k in range(len(real))],
        [out[PATCH:, k * PATCH : (k + 1) * PATCH] for k in range(len(real))],
    )


def column_place(col, own_first):
    block = col // PATCH
    near = block ^ own_first
    far = ((block + 1) % BLOCKS) ^ own_first
    return near, far, col % PATCH


def positions_kernel(
    from_strips,
    rows_hbm,
    cols_hbm,
    live_hbm,
    probe_ref,
    amps_hbm,
    tables_hbm,
    first_ref,
    mine_ref,
    other_ref,
    keep_up_ref,
    keep_low_ref,
    give_up_ref,
    give_low_ref,
    keep_probe_ref,
    give_probe_ref,
    probe_sums_ref,
    band,
    sums,
    amps_ref,
    tables,
    rows_ref,
    cols_ref,
    live_ref,
    sems,
    amp_sems,
):
    core = lax.axis_index("pos").astype(jnp.int32)
    here = lax.axis_index(TILE[2]).astype(jnp.int32)
    own_first = core * HALF

    def amp_copy(group):
        place = pl.ds(group * GROUP, GROUP)
        return pltpu.make_async_copy(amps_hbm.at[place], amps_ref.at[place], amp_sems.at[group])

    copies = [
        (tables_hbm, tables),
        (rows_hbm, rows_ref),
        (cols_hbm, cols_ref),
        (live_hbm, live_ref),
    ]
    if from_strips:
        for k in range(BLOCKS):
            start = pl.multiple_of((k ^ own_first) * PATCH, PATCH)
            copies.append((first_ref.at[:, :, pl.ds(start, PATCH)], band.at[:, k, :STRIP, :]))
            half = mine_ref if k < HALF else other_ref
            columns = pl.ds(k % HALF * PATCH, PATCH)
            copies.append((half.at[:, :, columns], band.at[:, k, STRIP:, :]))
    else:
        copies.append((mine_ref, band.at[:, :HALF]))
        copies.append((other_ref, band.at[:, HALF:]))
    started = [pltpu.make_async_copy(a, b, sems.at[n]) for n, (a, b) in enumerate(copies)]
    for copy in started:
        copy.start()
    amp_copy(0).start()
    sums[...] = jnp.zeros_like(sums)
    probe_sums_ref[...] = jnp.zeros_like(probe_sums_ref)
    for copy in started:
        copy.wait()
    live = live_ref[0, 0]
    lane = lax.broadcasted_iota(jnp.int32, (PATCH, PATCH), 1)

    steps = (live + GROUP - 1) // GROUP

    def visit(step, carry):
        amp_copy(step).wait()

        @pl.when(step + 1 < steps)
        def _():
            amp_copy(step + 1).start()

        slots = [step * GROUP + k for k in range(GROUP)]
        places = [column_place(cols_ref[0, 0, s], own_first) for s in slots]
        rows = [rows_ref[0, 0, s] for s in slots]
        patches = {}
        waves = {}

        def cut(pair):
            probe_real, probe_imag = probe_ref[0], probe_ref[1]
            real, imag = [], []
            for k in (2 * pair, 2 * pair + 1):
                near, far, shift = places[k]
                back = (PATCH - shift) % PATCH
                patch = []
                for plane in range(2):
                    a = band[plane, near, pl.ds(rows[k], PATCH), :]
                    b = band[plane, far, pl.ds(rows[k], PATCH), :]
                    patch.append(pltpu.roll(jnp.where(lane >= shift, a, b), back, 1))
                patches[k] = patch
                real.append(probe_real * patch[0] - probe_imag * patch[1])
                imag.append(probe_real * patch[1] + probe_imag * patch[0])
            waves[pair] = (real, imag)

        def rescale(pair):
            real, imag = waves[pair]
            for k in range(2):
                slot = slots[2 * pair + k]
                power = real[k] * real[k] + imag[k] * imag[k]
                ratio = jnp.where(slot < live, amps_ref[slot], 0.0) * lax.rsqrt(
                    jnp.maximum(power, MODULUS_FLOOR * MODULUS_FLOOR)
                )
                real[k] = real[k] * ratio
                imag[k] = imag[k] * ratio

        def right(pair, table):
            waves[pair] = times_right(*waves[pair], tables[table], tables[table + 1])

        def left(pair, table):
            waves[pair] = times_left(*waves[pair], tables[table], tables[table + 1])

        def collect(pair):
            probe_real, probe_imag = probe_ref[0], probe_ref[1]
            probe_power = probe_real * probe_real + probe_imag * probe_imag
            totals = [0.0, 0.0, 0.0]
            for back_real, back_imag, k in zip(*waves[pair], (2 * pair, 2 * pair + 1)):
                alive = slots[k] < live
                patch_real, patch_imag = patches[k]
                patch_power = patch_real * patch_real + patch_imag * patch_imag
                totals[0] += patch_real * back_real + patch_imag * back_imag
                totals[1] += patch_real * back_imag - patch_imag * back_real
                totals[2] += jnp.where(alive, patch_power, 0.0)
                near, far, shift = places[k]
                terms = (
                    probe_real * back_real + probe_imag * back_imag,
                    probe_real * back_imag - probe_imag * back_real,
                    jnp.where(alive, probe_power, 0.0),
                )
                inside = lane >= shift
                for plane in range(3):
                    turned = pltpu.roll(terms[plane], shift, 1)
                    sums[plane, near, pl.ds(rows[k], PATCH), :] += jnp.where(inside, turned, 0.0)
                    sums[plane, far, pl.ds(rows[k], PATCH), :] += jnp.where(inside, 0.0, turned)
            for plane in range(3):
                probe_sums_ref[pl.ds(plane * PATCH, PATCH), :] += totals[plane]

        stages = (
            cut,
            lambda pair: right(pair, 0),
            lambda pair: left(pair, 2),
            rescale,
            lambda pair: left(pair, 6),
            lambda pair: right(pair, 4),
            collect,
        )
        pairs = GROUP // 2
        for stage in stages:
            for pair in range(pairs):
                stage(pair)
        return carry

    lax.fori_loop(0, steps, visit, 0)
    outs = [
        (sums.at[:, HALF:, STRIP:, :], give_low_ref),
        (sums.at[:, HALF:, :STRIP, :], give_up_ref),
        (sums.at[:, :HALF, STRIP:, :], keep_low_ref),
        (sums.at[:, :HALF, :STRIP, :], keep_up_ref),
    ]
    count, height, _ = keep_probe_ref.shape
    for half, out in ((core, keep_probe_ref), (1 - core, give_probe_ref)):
        for k in range(count):
            start = (half * count + (here + k) % count) * height
            outs.append((probe_sums_ref.at[pl.ds(pl.multiple_of(start, 8), height)], out.at[k]))
    started = [pltpu.make_async_copy(a, b, sems.at[n]) for n, (a, b) in enumerate(outs)]
    for copy in started:
        copy.start()
    for copy in started:
        copy.wait()


def run_positions(scalars, probe, amps, tables, first, mine, other):
    from_strips = first is not None
    quarter = jax.ShapeDtypeStruct((3, HALF, STRIP, PATCH), jnp.float32)
    count = lax.axis_size(TILE[2])
    pieces_of = jax.ShapeDtypeStruct((count, 3 * PATCH // (2 * count), PATCH), jnp.float32)

    def kernel(*refs):
        if from_strips:
            positions_kernel(True, *refs)
        else:
            positions_kernel(False, *refs[:6], None, *refs[6:])

    pieces = (first, mine, other) if from_strips else (mine, other)
    return pl.pallas_call(
        kernel,
        out_shape=(quarter,) * 4 + (pieces_of,) * 2,
        in_specs=[ANY] * 3 + [VMEM] + [ANY] * (2 + len(pieces)),
        out_specs=(ANY,) * 6,
        scratch_shapes=[
            pltpu.VMEM((3 * PATCH, PATCH), jnp.float32),
            pltpu.VMEM((2, BLOCKS, BAND, PATCH), jnp.float32),
            pltpu.VMEM((3, BLOCKS, BAND, PATCH), jnp.float32),
            pltpu.VMEM(amps.shape, jnp.float32),
            pltpu.VMEM(tables.shape, tables.dtype),
            *(pltpu.SMEM(s.shape, jnp.int32) for s in scalars),
            pltpu.SemaphoreType.DMA((2 * BLOCKS + 4,)),
            pltpu.SemaphoreType.DMA((amps.shape[0] // GROUP,)),
        ],
        compiler_params=pltpu.CompilerParams(vmem_limit_bytes=60 * 2**20),
        cost_estimate=pl.CostEstimate(
            flops=13 * 10**9, bytes_accessed=8 * 2**20, transcendentals=2**19
        ),
        name="positions",
    )(*scalars, probe, amps, tables, *pieces)


def joined_over_cores(part):
    first = lax.axis_index("pos") == 0
    other = swapped(part)
    low = jnp.where(first, part, other)
    high = jnp.where(first, other, part)
    return jnp.concatenate([low, high])


def fans_of(count):
    fans = []
    stride = 1
    while stride < count:
        fans.append((stride, 4 if count % (stride * 4) == 0 else 2))
        stride *= fans[-1][1]
    return fans


def summed_over(part, axis):
    for stride, fan in fans_of(lax.axis_size(axis)):
        part = shifts_among(part, axis, stride, fan)
    return part


def moved_along(value, shift):
    depth, wide, high = (lax.axis_size(axis) for axis in TILE)
    route = []
    for place in range(depth * wide * high):
        line = place % (wide * high)
        step = shift if line == 0 else -shift
        route.append((place, (place // (wide * high) + step) % depth * wide * high + line))
    return lax.ppermute(value, TILE, route)


def summed_one_way(part):
    count = lax.axis_size(TILE[0])
    stride = 1
    while stride < count:
        part = part + moved_along(part, stride)
        stride *= 2
    return part


def scattered_over(pieces, axis):
    count = lax.axis_size(axis)
    arrived = []
    for step in range(1, count):
        route = [(i, (i + step) % count) for i in range(count)]
        arrived.append(lax.ppermute(pieces[step], axis, route))
    total = pieces[0]
    for piece in arrived:
        total = total + piece
    return total


def gathered_over(piece, axis):
    count = lax.axis_size(axis)
    here = lax.axis_index(axis)
    pieces = [piece]
    for step in range(1, count):
        pieces.append(lax.ppermute(piece, axis, [((i + step) % count, i) for i in range(count)]))
    rows = []
    for place in range(count):
        row = pieces[0]
        for step in range(1, count):
            row = jnp.where((place - here) % count == step, pieces[step], row)
        rows.append(row)
    return jnp.concatenate(rows)


def after(value, other):
    line = other[(0,) * (other.ndim - 1)][:PATCH]
    return value + jnp.minimum(jnp.abs(line), 0.0)


def shifts_among(value, axis, stride, fan):
    count = lax.axis_size(axis)
    total = value
    for step in range(1, fan):
        route = []
        for i in range(count):
            place = i // stride % fan
            route.append((i, i + ((place + step) % fan - place) * stride))
        total = total + lax.ppermute(value, axis, route)
    return total


def in_blocks(value):
    lines = value.reshape(*value.shape[:2], HALF, PATCH)
    return lines.transpose(0, 2, 1, 3)


def on_device(object_field, probe_field, amplitudes, scan_rows, scan_cols, live_count):
    tables = dft_tables()
    core = lax.axis_index("pos")
    amps = amplitudes[0, 0]
    scalars = (scan_rows, scan_cols, live_count)
    probe_relax = amps.shape[0] * lax.axis_size(TILE) * lax.axis_size("pos") / 4.0
    own_half = lax.dynamic_slice_in_dim(object_field, core * (COLS // 2), COLS // 2, 2)
    halo = from_tile(own_half, 1)
    halo_other = swapped(halo)
    up, low, give_up, give_low, keep_sums, give_sums = run_positions(
        scalars, probe_field, amps, tables, object_field, halo, halo_other
    )

    def next_probe(part, earlier, probe):
        part = gathered_over(part, TILE[2])
        if earlier is not None:
            part = after(part, earlier)
        total = joined_over_cores(part).reshape(3, PATCH, PATCH)
        return (total[:2] + probe_relax * probe) / (total[2] + probe_relax)[None]

    def updated(sums, field):
        return (sums[:2] + OBJECT_RELAX * field) / (sums[2] + OBJECT_RELAX)[None]

    part = scattered_over(keep_sums + swapped(give_sums), TILE[2])
    low = after(low + swapped(give_low), part)
    up = after(up + swapped(give_up), part)
    above = from_tile(low, -1)
    below = from_tile(up, 1)
    part = summed_over(summed_one_way(part), TILE[1])
    up, low, above, below = lax.optimization_barrier((up, low, above, below))
    own_half = updated(up + above, in_blocks(own_half))
    mine = jnp.concatenate([own_half, updated(low + below, in_blocks(halo))], axis=2)
    other = swapped(mine)
    probe_field = next_probe(part, None, probe_field)
    up, low, give_up, give_low, keep_sums, give_sums = run_positions(
        scalars, probe_field, amps, tables, None, mine, other
    )
    part = scattered_over(keep_sums + swapped(give_sums), TILE[2])
    low = after(low + swapped(give_low), part)
    up = up + swapped(give_up)
    above = from_tile(low, -1)
    part = summed_over(summed_one_way(part), TILE[1])
    up = after(up, part)
    mine = updated(up + above, own_half).transpose(0, 2, 1, 3).reshape(2, STRIP, COLS // 2)
    other = swapped(mine)
    left = jnp.where(core == 0, mine, other)
    right = jnp.where(core == 0, other, mine)
    object_out = jnp.concatenate([left, right], axis=2)
    probe_out = next_probe(part, object_out, probe_field)
    return object_out, probe_out


def torus_of(mesh):
    shape = (mesh.shape["tile"],)
    shape = (8, 4, 4) if shape == (128,) else (1, 1, *shape)
    return Mesh(mesh.devices.reshape(*shape, mesh.shape["pos"]), (*TILE, "pos"))


def solution(mesh):
    return jax.shard_map(
        on_device,
        mesh=torus_of(mesh),
        in_specs=(
            P(None, TILE, None),
            P(),
            P(TILE, "pos", None, None, None),
            P(TILE, "pos", None),
            P(TILE, "pos", None),
            P(TILE, "pos"),
        ),
        out_specs=(P(None, TILE, None), P()),
        check_vma=False,
    )
```

```python
import math

import jax
import jax.numpy as jnp
import numpy as np
from jax import lax
from jax.experimental import pallas as pl
from jax.experimental.pallas import tpu as pltpu
from jax.sharding import Mesh
from jax.sharding import PartitionSpec as P

PATCH = 128
STRIP = 128
COLS = 1024
BLOCKS = COLS // PATCH
HALF = BLOCKS // 2
BAND = 2 * STRIP
GROUP = 8
ITERS = 2
TILE = ("tile_0", "tile_1", "tile_2")
MODULUS_FLOOR = 0.2
OBJECT_RELAX = 1.0
ANY = pl.BlockSpec(memory_space=pl.ANY)


def swapped(value):
    return lax.ppermute(value, "pos", [(0, 1), (1, 0)])


def from_tile(value, distance):
    count = lax.axis_size(TILE)
    return lax.ppermute(value, TILE, [((i + distance) % count, i) for i in range(count)])


def two_terms(value):
    high = value.astype(jnp.bfloat16)
    low = (value - high.astype(jnp.float32)).astype(jnp.bfloat16)
    return high, low


def dft_tables():
    counter = np.arange(PATCH)
    angle = (counter[:, None] * counter[None, :] % PATCH) * (2.0 * math.pi / PATCH)
    cosine = np.cos(angle) / math.sqrt(PATCH)
    sine = np.sin(angle) / math.sqrt(PATCH)
    tables = []
    for sign in (1.0, -1.0):
        cross = sign * sine
        table = np.block([[cosine, -cross], [cross, cosine]]).astype(np.float32)
        high = table.astype(jnp.bfloat16)
        tables += [high, (table - high.astype(np.float32)).astype(jnp.bfloat16)]
    return jnp.asarray(np.stack(tables))


def times_right(real, imag, high_table, low_table):
    stacked = jnp.concatenate(
        [jnp.concatenate([r, i], axis=1) for r, i in zip(real, imag)], axis=0
    )
    high, low = two_terms(stacked)
    wide = jnp.concatenate([high, low, high], axis=1)
    table = jnp.concatenate([high_table, high_table, low_table], axis=0)
    out = jnp.dot(wide, table, preferred_element_type=jnp.float32)
    return (
        [out[k * PATCH : (k + 1) * PATCH, :PATCH] for k in range(len(real))],
        [out[k * PATCH : (k + 1) * PATCH, PATCH:] for k in range(len(real))],
    )


def times_left(real, imag, high_table, low_table):
    stacked = jnp.concatenate(
        [jnp.concatenate(real, axis=1), jnp.concatenate(imag, axis=1)], axis=0
    )
    high, low = two_terms(stacked)
    tall = jnp.concatenate([high, low, high], axis=0)
    table = jnp.concatenate([high_table, high_table, low_table], axis=1)
    out = jnp.dot(table, tall, preferred_element_type=jnp.float32)
    return (
        [out[:PATCH, k * PATCH : (k + 1) * PATCH] for k in range(len(real))],
        [out[PATCH:, k * PATCH : (k + 1) * PATCH] for k in range(len(real))],
    )


def column_place(col, own_first):
    block = col // PATCH
    near = block ^ own_first
    far = ((block + 1) % BLOCKS) ^ own_first
    return near, far, col % PATCH


def positions_kernel(
    from_strips,
    rows_hbm,
    cols_hbm,
    live_hbm,
    probe_hbm,
    amps_hbm,
    tables_hbm,
    first_ref,
    mine_ref,
    other_ref,
    keep_up_ref,
    keep_low_ref,
    give_up_ref,
    give_low_ref,
    keep_probe_ref,
    give_probe_ref,
    probe_sums_ref,
    band,
    sums,
    amps_ref,
    probe_ref,
    tables,
    rows_ref,
    cols_ref,
    live_ref,
    sems,
    amp_sems,
):
    core = lax.axis_index("pos").astype(jnp.int32)
    here = lax.axis_index(TILE[2]).astype(jnp.int32)
    own_first = core * HALF

    def amp_copy(group):
        place = pl.ds(group * GROUP, GROUP)
        return pltpu.make_async_copy(amps_hbm.at[place], amps_ref.at[place], amp_sems.at[group])

    copies = [
        (tables_hbm, tables),
        (probe_hbm, probe_ref),
        (rows_hbm, rows_ref),
        (cols_hbm, cols_ref),
        (live_hbm, live_ref),
    ]
    if from_strips:
        for k in range(BLOCKS):
            start = pl.multiple_of((k ^ own_first) * PATCH, PATCH)
            copies.append((first_ref.at[:, :, pl.ds(start, PATCH)], band.at[:, k, :STRIP, :]))
            half = mine_ref if k < HALF else other_ref
            columns = pl.ds(k % HALF * PATCH, PATCH)
            copies.append((half.at[:, :, columns], band.at[:, k, STRIP:, :]))
    else:
        copies.append((mine_ref, band.at[:, :HALF]))
        copies.append((other_ref, band.at[:, HALF:]))
    started = [pltpu.make_async_copy(a, b, sems.at[n]) for n, (a, b) in enumerate(copies)]
    for copy in started:
        copy.start()
    amp_copy(0).start()
    sums[...] = jnp.zeros_like(sums)
    probe_sums_ref[...] = jnp.zeros_like(probe_sums_ref)
    for copy in started:
        copy.wait()
    live = live_ref[0, 0]
    lane = lax.broadcasted_iota(jnp.int32, (PATCH, PATCH), 1)

    steps = (live + GROUP - 1) // GROUP

    def visit(step, carry):
        amp_copy(step).wait()

        @pl.when(step + 1 < steps)
        def _():
            amp_copy(step + 1).start()

        slots = [step * GROUP + k for k in range(GROUP)]
        places = [column_place(cols_ref[0, 0, s], own_first) for s in slots]
        rows = [rows_ref[0, 0, s] for s in slots]
        patches = {}
        waves = {}

        def cut(pair):
            probe_real, probe_imag = probe_ref[0], probe_ref[1]
            real, imag = [], []
            for k in (2 * pair, 2 * pair + 1):
                near, far, shift = places[k]
                back = (PATCH - shift) % PATCH
                patch = []
                for plane in range(2):
                    a = band[plane, near, pl.ds(rows[k], PATCH), :]
                    b = band[plane, far, pl.ds(rows[k], PATCH), :]
                    patch.append(pltpu.roll(jnp.where(lane >= shift, a, b), back, 1))
                patches[k] = patch
                real.append(probe_real * patch[0] - probe_imag * patch[1])
                imag.append(probe_real * patch[1] + probe_imag * patch[0])
            waves[pair] = (real, imag)

        def rescale(pair):
            real, imag = waves[pair]
            for k in range(2):
                slot = slots[2 * pair + k]
                power = real[k] * real[k] + imag[k] * imag[k]
                ratio = jnp.where(slot < live, amps_ref[slot], 0.0) * lax.rsqrt(
                    jnp.maximum(power, MODULUS_FLOOR * MODULUS_FLOOR)
                )
                real[k] = real[k] * ratio
                imag[k] = imag[k] * ratio

        def right(pair, table):
            waves[pair] = times_right(*waves[pair], tables[table], tables[table + 1])

        def left(pair, table):
            waves[pair] = times_left(*waves[pair], tables[table], tables[table + 1])

        def collect(pair):
            probe_real, probe_imag = probe_ref[0], probe_ref[1]
            probe_power = probe_real * probe_real + probe_imag * probe_imag
            totals = [0.0, 0.0, 0.0]
            for back_real, back_imag, k in zip(*waves[pair], (2 * pair, 2 * pair + 1)):
                alive = slots[k] < live
                patch_real, patch_imag = patches[k]
                patch_power = patch_real * patch_real + patch_imag * patch_imag
                totals[0] += patch_real * back_real + patch_imag * back_imag
                totals[1] += patch_real * back_imag - patch_imag * back_real
                totals[2] += jnp.where(alive, patch_power, 0.0)
                near, far, shift = places[k]
                terms = (
                    probe_real * back_real + probe_imag * back_imag,
                    probe_real * back_imag - probe_imag * back_real,
                    jnp.where(alive, probe_power, 0.0),
                )
                inside = lane >= shift
                for plane in range(3):
                    turned = pltpu.roll(terms[plane], shift, 1)
                    sums[plane, near, pl.ds(rows[k], PATCH), :] += jnp.where(inside, turned, 0.0)
                    sums[plane, far, pl.ds(rows[k], PATCH), :] += jnp.where(inside, 0.0, turned)
            for plane in range(3):
                probe_sums_ref[pl.ds(plane * PATCH, PATCH), :] += totals[plane]

        stages = (
            cut,
            lambda pair: right(pair, 0),
            lambda pair: left(pair, 2),
            rescale,
            lambda pair: left(pair, 0),
            lambda pair: right(pair, 2),
            collect,
        )
        pairs = GROUP // 2
        for stage in stages:
            for pair in range(pairs):
                stage(pair)
        return carry

    lax.fori_loop(0, steps, visit, 0)
    outs = [
        (sums.at[:, HALF:, STRIP:, :], give_low_ref),
        (sums.at[:, HALF:, :STRIP, :], give_up_ref),
        (sums.at[:, :HALF, STRIP:, :], keep_low_ref),
        (sums.at[:, :HALF, :STRIP, :], keep_up_ref),
    ]
    count, height, _ = keep_probe_ref.shape
    for half, out in ((core, keep_probe_ref), (1 - core, give_probe_ref)):
        for k in range(count):
            start = (half * count + (here + k) % count) * height
            outs.append((probe_sums_ref.at[pl.ds(pl.multiple_of(start, 8), height)], out.at[k]))
    started = [pltpu.make_async_copy(a, b, sems.at[n]) for n, (a, b) in enumerate(outs)]
    for copy in started:
        copy.start()
    for copy in started:
        copy.wait()


def run_positions(scalars, probe, amps, tables, first, mine, other):
    from_strips = first is not None
    quarter = jax.ShapeDtypeStruct((3, HALF, STRIP, PATCH), jnp.float32)
    count = lax.axis_size(TILE[2])
    pieces_of = jax.ShapeDtypeStruct((count, 3 * PATCH // (2 * count), PATCH), jnp.float32)

    def kernel(*refs):
        if from_strips:
            positions_kernel(True, *refs)
        else:
            positions_kernel(False, *refs[:6], None, *refs[6:])

    pieces = (first, mine, other) if from_strips else (mine, other)
    return pl.pallas_call(
        kernel,
        out_shape=(quarter,) * 4 + (pieces_of,) * 2,
        in_specs=[ANY] * (6 + len(pieces)),
        out_specs=(ANY,) * 6,
        scratch_shapes=[
            pltpu.VMEM((3 * PATCH, PATCH), jnp.float32),
            pltpu.VMEM((2, BLOCKS, BAND, PATCH), jnp.float32),
            pltpu.VMEM((3, BLOCKS, BAND, PATCH), jnp.float32),
            pltpu.VMEM(amps.shape, jnp.float32),
            pltpu.VMEM(probe.shape, jnp.float32),
            pltpu.VMEM(tables.shape, tables.dtype),
            *(pltpu.SMEM(s.shape, jnp.int32) for s in scalars),
            pltpu.SemaphoreType.DMA((2 * BLOCKS + 5,)),
            pltpu.SemaphoreType.DMA((amps.shape[0] // GROUP,)),
        ],
        compiler_params=pltpu.CompilerParams(vmem_limit_bytes=60 * 2**20),
        cost_estimate=pl.CostEstimate(
            flops=13 * 10**9, bytes_accessed=8 * 2**20, transcendentals=2**19
        ),
        name="positions",
    )(*scalars, probe, amps, tables, *pieces)


def joined_over_cores(part):
    first = lax.axis_index("pos") == 0
    other = swapped(part)
    low = jnp.where(first, part, other)
    high = jnp.where(first, other, part)
    return jnp.concatenate([low, high])


def fans_of(count):
    fans = []
    stride = 1
    while stride < count:
        fans.append((stride, 4 if count % (stride * 4) == 0 else 2))
        stride *= fans[-1][1]
    return fans


def summed_over(part, axis):
    for stride, fan in fans_of(lax.axis_size(axis)):
        part = shifts_among(part, axis, stride, fan)
    return part


def moved_along(value, shift):
    depth, wide, high = (lax.axis_size(axis) for axis in TILE)
    route = []
    for place in range(depth * wide * high):
        line = place % (wide * high)
        step = shift if line == 0 else -shift
        route.append((place, (place // (wide * high) + step) % depth * wide * high + line))
    return lax.ppermute(value, TILE, route)


def summed_one_way(part):
    count = lax.axis_size(TILE[0])
    stride = 1
    while stride < count:
        part = part + moved_along(part, stride)
        stride *= 2
    return part


def scattered_over(pieces, axis):
    count = lax.axis_size(axis)
    arrived = []
    for step in range(1, count):
        route = [(i, (i + step) % count) for i in range(count)]
        arrived.append(lax.ppermute(pieces[step], axis, route))
    total = pieces[0]
    for piece in arrived:
        total = total + piece
    return total


def gathered_over(piece, axis):
    count = lax.axis_size(axis)
    here = lax.axis_index(axis)
    pieces = [piece]
    for step in range(1, count):
        pieces.append(lax.ppermute(piece, axis, [((i + step) % count, i) for i in range(count)]))
    rows = []
    for place in range(count):
        row = pieces[0]
        for step in range(1, count):
            row = jnp.where((place - here) % count == step, pieces[step], row)
        rows.append(row)
    return jnp.concatenate(rows)


def after(value, other):
    line = other[(0,) * (other.ndim - 1)][:PATCH]
    return value + jnp.minimum(jnp.abs(line), 0.0)


def shifts_among(value, axis, stride, fan):
    count = lax.axis_size(axis)
    total = value
    for step in range(1, fan):
        route = []
        for i in range(count):
            place = i // stride % fan
            route.append((i, i + ((place + step) % fan - place) * stride))
        total = total + lax.ppermute(value, axis, route)
    return total


def in_blocks(value):
    lines = value.reshape(*value.shape[:2], HALF, PATCH)
    return lines.transpose(0, 2, 1, 3)


def on_device(object_field, probe_field, amplitudes, scan_rows, scan_cols, live_count):
    tables = dft_tables()
    core = lax.axis_index("pos")
    amps = amplitudes[0, 0]
    scalars = (scan_rows, scan_cols, live_count)
    probe_relax = amps.shape[0] * lax.axis_size(TILE) * lax.axis_size("pos") / 4.0
    own_half = lax.dynamic_slice_in_dim(object_field, core * (COLS // 2), COLS // 2, 2)
    halo = from_tile(own_half, 1)
    halo_other = swapped(halo)
    up, low, give_up, give_low, keep_sums, give_sums = run_positions(
        scalars, probe_field, amps, tables, object_field, halo, halo_other
    )

    def next_probe(part, earlier, probe):
        part = gathered_over(part, TILE[2])
        if earlier is not None:
            part = after(part, earlier)
        total = joined_over_cores(part).reshape(3, PATCH, PATCH)
        return (total[:2] + probe_relax * probe) / (total[2] + probe_relax)[None]

    def updated(sums, field):
        return (sums[:2] + OBJECT_RELAX * field) / (sums[2] + OBJECT_RELAX)[None]

    part = scattered_over(keep_sums + swapped(give_sums), TILE[2])
    low = after(low + swapped(give_low), part)
    up = after(up + swapped(give_up), part)
    above = from_tile(low, -1)
    below = from_tile(up, 1)
    part = summed_over(summed_one_way(part), TILE[1])
    up, low, above, below = lax.optimization_barrier((up, low, above, below))
    own_half = updated(up + above, in_blocks(own_half))
    mine = jnp.concatenate([own_half, updated(low + below, in_blocks(halo))], axis=2)
    other = swapped(mine)
    probe_field = next_probe(part, None, probe_field)
    up, low, give_up, give_low, keep_sums, give_sums = run_positions(
        scalars, probe_field, amps, tables, None, mine, other
    )
    part = scattered_over(keep_sums + swapped(give_sums), TILE[2])
    low = after(low + swapped(give_low), part)
    up = up + swapped(give_up)
    above = from_tile(low, -1)
    part = summed_over(summed_one_way(part), TILE[1])
    up = after(up, part)
    mine = updated(up + above, own_half).transpose(0, 2, 1, 3).reshape(2, STRIP, COLS // 2)
    other = swapped(mine)
    left = jnp.where(core == 0, mine, other)
    right = jnp.where(core == 0, other, mine)
    object_out = jnp.concatenate([left, right], axis=2)
    probe_out = next_probe(part, object_out, probe_field)
    return object_out, probe_out


def torus_of(mesh):
    shape = (mesh.shape["tile"],)
    shape = (8, 4, 4) if shape == (128,) else (1, 1, *shape)
    return Mesh(mesh.devices.reshape(*shape, mesh.shape["pos"]), (*TILE, "pos"))


def solution(mesh):
    return jax.shard_map(
        on_device,
        mesh=torus_of(mesh),
        in_specs=(
            P(None, TILE, None),
            P(),
            P(TILE, "pos", None, None, None),
            P(TILE, "pos", None),
            P(TILE, "pos", None),
            P(TILE, "pos"),
        ),
        out_specs=(P(None, TILE, None), P()),
        check_vma=False,
    )
```

```python
import math

import jax
import jax.numpy as jnp
import numpy as np
from jax import lax
from jax.experimental import pallas as pl
from jax.experimental.pallas import tpu as pltpu
from jax.sharding import Mesh
from jax.sharding import PartitionSpec as P

PATCH = 128
STRIP = 128
COLS = 1024
BLOCKS = COLS // PATCH
HALF = BLOCKS // 2
BAND = 2 * STRIP
GROUP = 8
ITERS = 2
TILE = ("tile_0", "tile_1", "tile_2")
MODULUS_FLOOR = 0.2
OBJECT_RELAX = 1.0
ANY = pl.BlockSpec(memory_space=pl.ANY)


def swapped(value):
    return lax.ppermute(value, "pos", [(0, 1), (1, 0)])


def from_tile(value, distance):
    count = lax.axis_size(TILE)
    return lax.ppermute(value, TILE, [((i + distance) % count, i) for i in range(count)])


def two_terms(value):
    high = value.astype(jnp.bfloat16)
    low = (value - high.astype(jnp.float32)).astype(jnp.bfloat16)
    return high, low


def dft_tables():
    counter = np.arange(PATCH)
    angle = (counter[:, None] * counter[None, :] % PATCH) * (2.0 * math.pi / PATCH)
    cosine = np.cos(angle) / math.sqrt(PATCH)
    sine = np.sin(angle) / math.sqrt(PATCH)
    tables = []
    for sign in (1.0, -1.0):
        cross = sign * sine
        table = np.block([[cosine, -cross], [cross, cosine]]).astype(np.float32)
        high = table.astype(jnp.bfloat16)
        tables += [high, (table - high.astype(np.float32)).astype(jnp.bfloat16)]
    return jnp.asarray(np.stack(tables))


def times_right(real, imag, high_table, low_table):
    stacked = jnp.concatenate(
        [jnp.concatenate([r, i], axis=1) for r, i in zip(real, imag)], axis=0
    )
    high, low = two_terms(stacked)
    wide = jnp.concatenate([high, low, high], axis=1)
    table = jnp.concatenate([high_table, high_table, low_table], axis=0)
    out = jnp.dot(wide, table, preferred_element_type=jnp.float32)
    return (
        [out[k * PATCH : (k + 1) * PATCH, :PATCH] for k in range(len(real))],
        [out[k * PATCH : (k + 1) * PATCH, PATCH:] for k in range(len(real))],
    )


def times_left(real, imag, high_table, low_table):
    stacked = jnp.concatenate(
        [jnp.concatenate(real, axis=1), jnp.concatenate(imag, axis=1)], axis=0
    )
    high, low = two_terms(stacked)
    tall = jnp.concatenate([high, low, high], axis=0)
    table = jnp.concatenate([high_table, high_table, low_table], axis=1)
    out = jnp.dot(table, tall, preferred_element_type=jnp.float32)
    return (
        [out[:PATCH, k * PATCH : (k + 1) * PATCH] for k in range(len(real))],
        [out[PATCH:, k * PATCH : (k + 1) * PATCH] for k in range(len(real))],
    )


def column_place(col, own_first):
    block = col // PATCH
    near = block ^ own_first
    far = ((block + 1) % BLOCKS) ^ own_first
    return near, far, col % PATCH


def positions_kernel(
    from_strips,
    rows_hbm,
    cols_hbm,
    live_hbm,
    probe_hbm,
    amps_hbm,
    tables_hbm,
    first_ref,
    mine_ref,
    other_ref,
    keep_up_ref,
    keep_low_ref,
    give_up_ref,
    give_low_ref,
    keep_probe_ref,
    give_probe_ref,
    probe_sums_ref,
    band,
    sums,
    amps_ref,
    probe_ref,
    tables,
    rows_ref,
    cols_ref,
    live_ref,
    sems,
    amp_sems,
):
    core = lax.axis_index("pos").astype(jnp.int32)
    here = lax.axis_index(TILE[2]).astype(jnp.int32)
    own_first = core * HALF

    def amp_copy(group):
        place = pl.ds(group * GROUP, GROUP)
        return pltpu.make_async_copy(amps_hbm.at[place], amps_ref.at[place], amp_sems.at[group])

    copies = [
        (tables_hbm, tables),
        (probe_hbm, probe_ref),
        (rows_hbm, rows_ref),
        (cols_hbm, cols_ref),
        (live_hbm, live_ref),
    ]
    if from_strips:
        for k in range(BLOCKS):
            start = pl.multiple_of((k ^ own_first) * PATCH, PATCH)
            copies.append((first_ref.at[:, :, pl.ds(start, PATCH)], band.at[:, k, :STRIP, :]))
            half = mine_ref if k < HALF else other_ref
            columns = pl.ds(k % HALF * PATCH, PATCH)
            copies.append((half.at[:, :, columns], band.at[:, k, STRIP:, :]))
    else:
        copies.append((mine_ref, band.at[:, :HALF]))
        copies.append((other_ref, band.at[:, HALF:]))
    started = [pltpu.make_async_copy(a, b, sems.at[n]) for n, (a, b) in enumerate(copies)]
    for copy in started:
        copy.start()
    amp_copy(0).start()
    sums[...] = jnp.zeros_like(sums)
    probe_sums_ref[...] = jnp.zeros_like(probe_sums_ref)
    for copy in started:
        copy.wait()
    live = live_ref[0, 0]
    lane = lax.broadcasted_iota(jnp.int32, (PATCH, PATCH), 1)

    steps = (live + GROUP - 1) // GROUP

    def visit(step, carry):
        amp_copy(step).wait()

        @pl.when(step + 1 < steps)
        def _():
            amp_copy(step + 1).start()

        slots = [step * GROUP + k for k in range(GROUP)]
        places = [column_place(cols_ref[0, 0, s], own_first) for s in slots]
        rows = [rows_ref[0, 0, s] for s in slots]
        patches = {}
        waves = {}

        def cut(pair):
            probe_real, probe_imag = probe_ref[0], probe_ref[1]
            real, imag = [], []
            for k in (2 * pair, 2 * pair + 1):
                near, far, shift = places[k]
                back = (PATCH - shift) % PATCH
                patch = []
                for plane in range(2):
                    a = band[plane, near, pl.ds(rows[k], PATCH), :]
                    b = band[plane, far, pl.ds(rows[k], PATCH), :]
                    patch.append(pltpu.roll(jnp.where(lane >= shift, a, b), back, 1))
                patches[k] = patch
                real.append(probe_real * patch[0] - probe_imag * patch[1])
                imag.append(probe_real * patch[1] + probe_imag * patch[0])
            waves[pair] = (real, imag)

        def rescale(pair):
            real, imag = waves[pair]
            for k in range(2):
                slot = slots[2 * pair + k]
                power = real[k] * real[k] + imag[k] * imag[k]
                ratio = jnp.where(slot < live, amps_ref[slot], 0.0) * lax.rsqrt(
                    jnp.maximum(power, MODULUS_FLOOR * MODULUS_FLOOR)
                )
                real[k] = real[k] * ratio
                imag[k] = imag[k] * ratio

        def right(pair, table):
            waves[pair] = times_right(*waves[pair], tables[table], tables[table + 1])

        def left(pair, table):
            waves[pair] = times_left(*waves[pair], tables[table], tables[table + 1])

        def collect(pair):
            probe_real, probe_imag = probe_ref[0], probe_ref[1]
            probe_power = probe_real * probe_real + probe_imag * probe_imag
            totals = [0.0, 0.0, 0.0]
            for back_real, back_imag, k in zip(*waves[pair], (2 * pair, 2 * pair + 1)):
                alive = slots[k] < live
                patch_real, patch_imag = patches[k]
                patch_power = patch_real * patch_real + patch_imag * patch_imag
                totals[0] += patch_real * back_real + patch_imag * back_imag
                totals[1] += patch_real * back_imag - patch_imag * back_real
                totals[2] += jnp.where(alive, patch_power, 0.0)
                near, far, shift = places[k]
                terms = (
                    probe_real * back_real + probe_imag * back_imag,
                    probe_real * back_imag - probe_imag * back_real,
                    jnp.where(alive, probe_power, 0.0),
                )
                inside = lane >= shift
                for plane in range(3):
                    turned = pltpu.roll(terms[plane], shift, 1)
                    sums[plane, near, pl.ds(rows[k], PATCH), :] += jnp.where(inside, turned, 0.0)
                    sums[plane, far, pl.ds(rows[k], PATCH), :] += jnp.where(inside, 0.0, turned)
            for plane in range(3):
                probe_sums_ref[pl.ds(plane * PATCH, PATCH), :] += totals[plane]

        stages = (
            cut,
            lambda pair: right(pair, 0),
            lambda pair: left(pair, 2),
            rescale,
            lambda pair: left(pair, 0),
            lambda pair: right(pair, 2),
            collect,
        )
        pairs = GROUP // 2
        for stage in stages:
            for pair in range(pairs):
                stage(pair)
        return carry

    lax.fori_loop(0, steps, visit, 0)
    outs = [
        (sums.at[:, HALF:, STRIP:, :], give_low_ref),
        (sums.at[:, HALF:, :STRIP, :], give_up_ref),
        (sums.at[:, :HALF, STRIP:, :], keep_low_ref),
        (sums.at[:, :HALF, :STRIP, :], keep_up_ref),
    ]
    count, height, _ = keep_probe_ref.shape
    for half, out in ((core, keep_probe_ref), (1 - core, give_probe_ref)):
        for k in range(count):
            start = (half * count + (here + k) % count) * height
            outs.append((probe_sums_ref.at[pl.ds(pl.multiple_of(start, 8), height)], out.at[k]))
    started = [pltpu.make_async_copy(a, b, sems.at[n]) for n, (a, b) in enumerate(outs)]
    for copy in started:
        copy.start()
    for copy in started:
        copy.wait()


def run_positions(scalars, probe, amps, tables, first, mine, other):
    from_strips = first is not None
    quarter = jax.ShapeDtypeStruct((3, HALF, STRIP, PATCH), jnp.float32)
    count = lax.axis_size(TILE[2])
    pieces_of = jax.ShapeDtypeStruct((count, 3 * PATCH // (2 * count), PATCH), jnp.float32)

    def kernel(*refs):
        if from_strips:
            positions_kernel(True, *refs)
        else:
            positions_kernel(False, *refs[:6], None, *refs[6:])

    pieces = (first, mine, other) if from_strips else (mine, other)
    return pl.pallas_call(
        kernel,
        out_shape=(quarter,) * 4 + (pieces_of,) * 2,
        in_specs=[ANY] * (6 + len(pieces)),
        out_specs=(ANY,) * 6,
        scratch_shapes=[
            pltpu.VMEM((3 * PATCH, PATCH), jnp.float32),
            pltpu.VMEM((2, BLOCKS, BAND, PATCH), jnp.float32),
            pltpu.VMEM((3, BLOCKS, BAND, PATCH), jnp.float32),
            pltpu.VMEM(amps.shape, jnp.float32),
            pltpu.VMEM(probe.shape, jnp.float32),
            pltpu.VMEM(tables.shape, tables.dtype),
            *(pltpu.SMEM(s.shape, jnp.int32) for s in scalars),
            pltpu.SemaphoreType.DMA((2 * BLOCKS + 5,)),
            pltpu.SemaphoreType.DMA((amps.shape[0] // GROUP,)),
        ],
        compiler_params=pltpu.CompilerParams(vmem_limit_bytes=60 * 2**20),
        cost_estimate=pl.CostEstimate(
            flops=13 * 10**9, bytes_accessed=8 * 2**20, transcendentals=2**19
        ),
        name="positions",
    )(*scalars, probe, amps, tables, *pieces)


def joined_over_cores(part):
    first = lax.axis_index("pos") == 0
    other = swapped(part)
    low = jnp.where(first, part, other)
    high = jnp.where(first, other, part)
    return jnp.concatenate([low, high])


def fans_of(count):
    fans = []
    stride = 1
    while stride < count:
        fans.append((stride, 4 if count % (stride * 4) == 0 else 2))
        stride *= fans[-1][1]
    return fans


def summed_over(part, axis):
    for stride, fan in fans_of(lax.axis_size(axis)):
        part = shifts_among(part, axis, stride, fan)
    return part


def moved_along(value, shift):
    depth, wide, high = (lax.axis_size(axis) for axis in TILE)
    route = []
    for place in range(depth * wide * high):
        line = place % (wide * high)
        step = shift if line == 0 else -shift
        route.append((place, (place // (wide * high) + step) % depth * wide * high + line))
    return lax.ppermute(value, TILE, route)


def summed_one_way(part):
    count = lax.axis_size(TILE[0])
    stride = 1
    while stride < count:
        part = part + moved_along(part, stride)
        stride *= 2
    return part


def scattered_over(own, given, axis):
    count = lax.axis_size(axis)
    pieces = [own[step] + given[step] for step in range(count)]
    arrived = []
    for step in range(1, count):
        route = [(i, (i + step) % count) for i in range(count)]
        arrived.append(lax.ppermute(pieces[step], axis, route))
    total = pieces[0]
    for piece in arrived:
        total = total + piece
    return total


def gathered_over(piece, axis):
    count = lax.axis_size(axis)
    here = lax.axis_index(axis)
    pieces = [piece]
    for step in range(1, count):
        pieces.append(lax.ppermute(piece, axis, [((i + step) % count, i) for i in range(count)]))
    rows = []
    for place in range(count):
        row = pieces[0]
        for step in range(1, count):
            row = jnp.where((place - here) % count == step, pieces[step], row)
        rows.append(row)
    return jnp.concatenate(rows)


def after(value, other):
    line = other[(0,) * (other.ndim - 1)][:PATCH]
    return value + jnp.minimum(jnp.abs(line), 0.0)


def shifts_among(value, axis, stride, fan):
    count = lax.axis_size(axis)
    total = value
    for step in range(1, fan):
        route = []
        for i in range(count):
            place = i // stride % fan
            route.append((i, i + ((place + step) % fan - place) * stride))
        total = total + lax.ppermute(value, axis, route)
    return total


def in_blocks(value):
    lines = value.reshape(*value.shape[:2], HALF, PATCH)
    return lines.transpose(0, 2, 1, 3)


def on_device(object_field, probe_field, amplitudes, scan_rows, scan_cols, live_count):
    tables = dft_tables()
    core = lax.axis_index("pos")
    amps = amplitudes[0, 0]
    scalars = (scan_rows, scan_cols, live_count)
    probe_relax = amps.shape[0] * lax.axis_size(TILE) * lax.axis_size("pos") / 4.0
    own_half = lax.dynamic_slice_in_dim(object_field, core * (COLS // 2), COLS // 2, 2)
    halo = from_tile(own_half, 1)
    halo_other = swapped(halo)
    up, low, give_up, give_low, keep_sums, give_sums = run_positions(
        scalars, probe_field, amps, tables, object_field, halo, halo_other
    )

    def next_probe(part, earlier, probe):
        part = gathered_over(part, TILE[2])
        if earlier is not None:
            part = after(part, earlier)
        total = joined_over_cores(part).reshape(3, PATCH, PATCH)
        return (total[:2] + probe_relax * probe) / (total[2] + probe_relax)[None]

    def updated(sums, field):
        return (sums[:2] + OBJECT_RELAX * field) / (sums[2] + OBJECT_RELAX)[None]

    part = scattered_over(keep_sums, swapped(give_sums), TILE[2])
    low = after(low + swapped(give_low), part)
    up = after(up + swapped(give_up), part)
    above = from_tile(low, -1)
    below = from_tile(up, 1)
    part = summed_over(summed_one_way(part), TILE[1])
    up, low, above, below = lax.optimization_barrier((up, low, above, below))
    own_half = updated(up + above, in_blocks(own_half))
    mine = jnp.concatenate([own_half, updated(low + below, in_blocks(halo))], axis=2)
    other = swapped(mine)
    probe_field = next_probe(part, None, probe_field)
    up, low, give_up, give_low, keep_sums, give_sums = run_positions(
        scalars, probe_field, amps, tables, None, mine, other
    )
    part = scattered_over(keep_sums, swapped(give_sums), TILE[2])
    low = after(low + swapped(give_low), part)
    up = up + swapped(give_up)
    above = from_tile(low, -1)
    part = summed_over(summed_one_way(part), TILE[1])
    up = after(up, part)
    mine = updated(up + above, own_half).transpose(0, 2, 1, 3).reshape(2, STRIP, COLS // 2)
    other = swapped(mine)
    left = jnp.where(core == 0, mine, other)
    right = jnp.where(core == 0, other, mine)
    object_out = jnp.concatenate([left, right], axis=2)
    probe_out = next_probe(part, object_out, probe_field)
    return object_out, probe_out


def torus_of(mesh):
    shape = (mesh.shape["tile"],)
    shape = (8, 4, 4) if shape == (128,) else (1, 1, *shape)
    return Mesh(mesh.devices.reshape(*shape, mesh.shape["pos"]), (*TILE, "pos"))


def solution(mesh):
    return jax.shard_map(
        on_device,
        mesh=torus_of(mesh),
        in_specs=(
            P(None, TILE, None),
            P(),
            P(TILE, "pos", None, None, None),
            P(TILE, "pos", None),
            P(TILE, "pos", None),
            P(TILE, "pos"),
        ),
        out_specs=(P(None, TILE, None), P()),
        check_vma=False,
    )
```

```python
import math

import jax
import jax.numpy as jnp
import numpy as np
from jax import lax
from jax.experimental import pallas as pl
from jax.experimental.pallas import tpu as pltpu
from jax.sharding import Mesh
from jax.sharding import PartitionSpec as P

PATCH = 128
STRIP = 128
COLS = 1024
BLOCKS = COLS // PATCH
HALF = BLOCKS // 2
BAND = 2 * STRIP
GROUP = 8
ITERS = 2
TILE = ("tile_0", "tile_1", "tile_2")
MODULUS_FLOOR = 0.2
OBJECT_RELAX = 1.0
ANY = pl.BlockSpec(memory_space=pl.ANY)


def swapped(value):
    return lax.ppermute(value, "pos", [(0, 1), (1, 0)])


def from_tile(value, distance):
    count = lax.axis_size(TILE)
    return lax.ppermute(value, TILE, [((i + distance) % count, i) for i in range(count)])


def two_terms(value):
    high = value.astype(jnp.bfloat16)
    low = (value - high.astype(jnp.float32)).astype(jnp.bfloat16)
    return high, low


def dft_tables():
    counter = np.arange(PATCH)
    angle = (counter[:, None] * counter[None, :] % PATCH) * (2.0 * math.pi / PATCH)
    cosine = np.cos(angle) / math.sqrt(PATCH)
    sine = np.sin(angle) / math.sqrt(PATCH)
    tables = []
    for sign in (1.0, -1.0):
        cross = sign * sine
        table = np.block([[cosine, -cross], [cross, cosine]]).astype(np.float32)
        high = table.astype(jnp.bfloat16)
        tables += [high, (table - high.astype(np.float32)).astype(jnp.bfloat16)]
    return jnp.asarray(np.stack(tables))


def times_right(real, imag, high_table, low_table):
    stacked = jnp.concatenate(
        [jnp.concatenate([r, i], axis=1) for r, i in zip(real, imag)], axis=0
    )
    high, low = two_terms(stacked)
    wide = jnp.concatenate([high, low, high], axis=1)
    table = jnp.concatenate([high_table, high_table, low_table], axis=0)
    out = jnp.dot(wide, table, preferred_element_type=jnp.float32)
    return (
        [out[k * PATCH : (k + 1) * PATCH, :PATCH] for k in range(len(real))],
        [out[k * PATCH : (k + 1) * PATCH, PATCH:] for k in range(len(real))],
    )


def times_left(real, imag, high_table, low_table):
    stacked = jnp.concatenate(
        [jnp.concatenate(real, axis=1), jnp.concatenate(imag, axis=1)], axis=0
    )
    high, low = two_terms(stacked)
    tall = jnp.concatenate([high, low, high], axis=0)
    table = jnp.concatenate([high_table, high_table, low_table], axis=1)
    out = jnp.dot(table, tall, preferred_element_type=jnp.float32)
    return (
        [out[:PATCH, k * PATCH : (k + 1) * PATCH] for k in range(len(real))],
        [out[PATCH:, k * PATCH : (k + 1) * PATCH] for k in range(len(real))],
    )


def column_place(col, own_first):
    block = col // PATCH
    near = block ^ own_first
    far = ((block + 1) % BLOCKS) ^ own_first
    return near, far, col % PATCH


def positions_kernel(
    from_strips,
    rows_hbm,
    cols_hbm,
    live_hbm,
    probe_hbm,
    amps_hbm,
    tables_hbm,
    first_ref,
    mine_ref,
    other_ref,
    keep_up_ref,
    keep_low_ref,
    give_up_ref,
    give_low_ref,
    keep_probe_ref,
    give_probe_ref,
    probe_sums_ref,
    band,
    sums,
    amps_ref,
    probe_ref,
    tables,
    rows_ref,
    cols_ref,
    live_ref,
    sems,
    amp_sems,
):
    core = lax.axis_index("pos").astype(jnp.int32)
    here = lax.axis_index(TILE[2]).astype(jnp.int32)
    own_first = core * HALF

    def amp_copy(group):
        place = pl.ds(group * GROUP, GROUP)
        return pltpu.make_async_copy(amps_hbm.at[place], amps_ref.at[place], amp_sems.at[group])

    copies = [
        (tables_hbm, tables),
        (probe_hbm, probe_ref),
        (rows_hbm, rows_ref),
        (cols_hbm, cols_ref),
        (live_hbm, live_ref),
    ]
    if from_strips:
        for k in range(BLOCKS):
            start = pl.multiple_of((k ^ own_first) * PATCH, PATCH)
            copies.append((first_ref.at[:, :, pl.ds(start, PATCH)], band.at[:, k, :STRIP, :]))
            half = mine_ref if k < HALF else other_ref
            columns = pl.ds(k % HALF * PATCH, PATCH)
            copies.append((half.at[:, :, columns], band.at[:, k, STRIP:, :]))
    else:
        copies.append((mine_ref, band.at[:, :HALF]))
        copies.append((other_ref, band.at[:, HALF:]))
    started = [pltpu.make_async_copy(a, b, sems.at[n]) for n, (a, b) in enumerate(copies)]
    for copy in started:
        copy.start()
    amp_copy(0).start()
    sums[...] = jnp.zeros_like(sums)
    probe_sums_ref[...] = jnp.zeros_like(probe_sums_ref)
    for copy in started:
        copy.wait()
    live = live_ref[0, 0]
    lane = lax.broadcasted_iota(jnp.int32, (PATCH, PATCH), 1)

    steps = (live + GROUP - 1) // GROUP

    def visit(step, carry):
        amp_copy(step).wait()

        @pl.when(step + 1 < steps)
        def _():
            amp_copy(step + 1).start()

        slots = [step * GROUP + k for k in range(GROUP)]
        places = [column_place(cols_ref[0, 0, s], own_first) for s in slots]
        rows = [rows_ref[0, 0, s] for s in slots]
        patches = {}
        waves = {}

        def cut(pair):
            probe_real, probe_imag = probe_ref[0], probe_ref[1]
            real, imag = [], []
            for k in (2 * pair, 2 * pair + 1):
                near, far, shift = places[k]
                back = (PATCH - shift) % PATCH
                patch = []
                for plane in range(2):
                    a = band[plane, near, pl.ds(rows[k], PATCH), :]
                    b = band[plane, far, pl.ds(rows[k], PATCH), :]
                    patch.append(pltpu.roll(jnp.where(lane >= shift, a, b), back, 1))
                patches[k] = patch
                real.append(probe_real * patch[0] - probe_imag * patch[1])
                imag.append(probe_real * patch[1] + probe_imag * patch[0])
            waves[pair] = (real, imag)

        def rescale(pair):
            real, imag = waves[pair]
            for k in range(2):
                slot = slots[2 * pair + k]
                power = real[k] * real[k] + imag[k] * imag[k]
                ratio = jnp.where(slot < live, amps_ref[slot], 0.0) * lax.rsqrt(
                    jnp.maximum(power, MODULUS_FLOOR * MODULUS_FLOOR)
                )
                real[k] = real[k] * ratio
                imag[k] = imag[k] * ratio

        def right(pair, table):
            waves[pair] = times_right(*waves[pair], tables[table], tables[table + 1])

        def left(pair, table):
            waves[pair] = times_left(*waves[pair], tables[table], tables[table + 1])

        def collect(pair):
            probe_real, probe_imag = probe_ref[0], probe_ref[1]
            probe_power = probe_real * probe_real + probe_imag * probe_imag
            totals = [0.0, 0.0, 0.0]
            for back_real, back_imag, k in zip(*waves[pair], (2 * pair, 2 * pair + 1)):
                alive = slots[k] < live
                patch_real, patch_imag = patches[k]
                patch_power = patch_real * patch_real + patch_imag * patch_imag
                totals[0] += patch_real * back_real + patch_imag * back_imag
                totals[1] += patch_real * back_imag - patch_imag * back_real
                totals[2] += jnp.where(alive, patch_power, 0.0)
                near, far, shift = places[k]
                terms = (
                    probe_real * back_real + probe_imag * back_imag,
                    probe_real * back_imag - probe_imag * back_real,
                    jnp.where(alive, probe_power, 0.0),
                )
                inside = lane >= shift
                for plane in range(3):
                    turned = pltpu.roll(terms[plane], shift, 1)
                    sums[plane, near, pl.ds(rows[k], PATCH), :] += jnp.where(inside, turned, 0.0)
                    sums[plane, far, pl.ds(rows[k], PATCH), :] += jnp.where(inside, 0.0, turned)
            for plane in range(3):
                probe_sums_ref[pl.ds(plane * PATCH, PATCH), :] += totals[plane]

        stages = (
            cut,
            lambda pair: right(pair, 0),
            lambda pair: left(pair, 2),
            rescale,
            lambda pair: left(pair, 0),
            lambda pair: right(pair, 2),
            collect,
        )
        pairs = GROUP // 2
        for stage in stages:
            for pair in range(pairs):
                stage(pair)
        return carry

    lax.fori_loop(0, steps, visit, 0)
    outs = [
        (sums.at[:, HALF:, STRIP:, :], give_low_ref),
        (sums.at[:, HALF:, :STRIP, :], give_up_ref),
        (sums.at[:, :HALF, STRIP:, :], keep_low_ref),
        (sums.at[:, :HALF, :STRIP, :], keep_up_ref),
    ]
    count, height, _ = keep_probe_ref.shape
    for half, out in ((core, keep_probe_ref), (1 - core, give_probe_ref)):
        for k in range(count):
            start = (half * count + (here + k) % count) * height
            outs.append((probe_sums_ref.at[pl.ds(pl.multiple_of(start, 8), height)], out.at[k]))
    started = [pltpu.make_async_copy(a, b, sems.at[n]) for n, (a, b) in enumerate(outs)]
    for copy in started:
        copy.start()
    for copy in started:
        copy.wait()


def run_positions(scalars, probe, amps, tables, first, mine, other):
    from_strips = first is not None
    quarter = jax.ShapeDtypeStruct((3, HALF, STRIP, PATCH), jnp.float32)
    count = lax.axis_size(TILE[2])
    pieces_of = jax.ShapeDtypeStruct((count, 3 * PATCH // (2 * count), PATCH), jnp.float32)

    def kernel(*refs):
        if from_strips:
            positions_kernel(True, *refs)
        else:
            positions_kernel(False, *refs[:6], None, *refs[6:])

    pieces = (first, mine, other) if from_strips else (mine, other)
    return pl.pallas_call(
        kernel,
        out_shape=(quarter,) * 4 + (pieces_of,) * 2,
        in_specs=[ANY] * (6 + len(pieces)),
        out_specs=(ANY,) * 6,
        scratch_shapes=[
            pltpu.VMEM((3 * PATCH, PATCH), jnp.float32),
            pltpu.VMEM((2, BLOCKS, BAND, PATCH), jnp.float32),
            pltpu.VMEM((3, BLOCKS, BAND, PATCH), jnp.float32),
            pltpu.VMEM(amps.shape, jnp.float32),
            pltpu.VMEM(probe.shape, jnp.float32),
            pltpu.VMEM(tables.shape, tables.dtype),
            *(pltpu.SMEM(s.shape, jnp.int32) for s in scalars),
            pltpu.SemaphoreType.DMA((2 * BLOCKS + 5,)),
            pltpu.SemaphoreType.DMA((amps.shape[0] // GROUP,)),
        ],
        compiler_params=pltpu.CompilerParams(vmem_limit_bytes=60 * 2**20),
        cost_estimate=pl.CostEstimate(
            flops=13 * 10**9, bytes_accessed=8 * 2**20, transcendentals=2**19
        ),
        name="positions",
    )(*scalars, probe, amps, tables, *pieces)


def joined_over_cores(part):
    first = lax.axis_index("pos") == 0
    other = swapped(part)
    low = jnp.where(first, part, other)
    high = jnp.where(first, other, part)
    return jnp.concatenate([low, high])


def fans_of(count):
    fans = []
    stride = 1
    while stride < count:
        fans.append((stride, 4 if count % (stride * 4) == 0 else 2))
        stride *= fans[-1][1]
    return fans


def summed_over(part, axis):
    for stride, fan in fans_of(lax.axis_size(axis)):
        part = shifts_among(part, axis, stride, fan)
    return part


def moved_along(value, shift):
    depth, wide, high = (lax.axis_size(axis) for axis in TILE)
    route = []
    for place in range(depth * wide * high):
        line = place % (wide * high)
        step = shift if line == 0 else -shift
        route.append((place, (place // (wide * high) + step) % depth * wide * high + line))
    return lax.ppermute(value, TILE, route)


def summed_one_way(part):
    count = lax.axis_size(TILE[0])
    stride = 1
    while stride < count:
        part = part + moved_along(part, stride)
        stride *= 2
    return part


def scattered_over(pieces, axis):
    count = lax.axis_size(axis)
    arrived = []
    for step in range(1, count):
        route = [(i, (i + step) % count) for i in range(count)]
        arrived.append(lax.ppermute(pieces[step], axis, route))
    total = pieces[0]
    for piece in arrived:
        total = total + piece
    return total


def gathered_over(piece, axis):
    count = lax.axis_size(axis)
    here = lax.axis_index(axis)
    pieces = [piece]
    for step in range(1, count):
        pieces.append(lax.ppermute(piece, axis, [((i + step) % count, i) for i in range(count)]))
    rows = []
    for place in range(count):
        row = pieces[0]
        for step in range(1, count):
            row = jnp.where((place - here) % count == step, pieces[step], row)
        rows.append(row)
    return jnp.concatenate(rows)


def after(value, other):
    line = other[(0,) * (other.ndim - 1)][:PATCH]
    return value + jnp.minimum(jnp.abs(line), 0.0)


def shifts_among(value, axis, stride, fan):
    count = lax.axis_size(axis)
    total = value
    for step in range(1, fan):
        route = []
        for i in range(count):
            place = i // stride % fan
            route.append((i, i + ((place + step) % fan - place) * stride))
        total = total + lax.ppermute(value, axis, route)
    return total


def in_blocks(value):
    lines = value.reshape(*value.shape[:2], HALF, PATCH)
    return lines.transpose(0, 2, 1, 3)


def on_device(object_field, probe_field, amplitudes, scan_rows, scan_cols, live_count):
    tables = dft_tables()
    core = lax.axis_index("pos")
    amps = amplitudes[0, 0]
    scalars = (scan_rows, scan_cols, live_count)
    probe_relax = amps.shape[0] * lax.axis_size(TILE) * lax.axis_size("pos") / 4.0
    own_half = lax.dynamic_slice_in_dim(object_field, core * (COLS // 2), COLS // 2, 2)
    halo = from_tile(own_half, 1)
    halo_other = swapped(halo)
    up, low, give_up, give_low, keep_sums, give_sums = run_positions(
        scalars, probe_field, amps, tables, object_field, halo, halo_other
    )

    def next_probe(part, earlier, probe):
        part = gathered_over(part, TILE[2])
        if earlier is not None:
            part = after(part, earlier)
        total = joined_over_cores(part).reshape(3, PATCH, PATCH)
        return (total[:2] + probe_relax * probe) / (total[2] + probe_relax)[None]

    def updated(sums, field):
        return (sums[:2] + OBJECT_RELAX * field) / (sums[2] + OBJECT_RELAX)[None]

    part = scattered_over(keep_sums + swapped(give_sums), TILE[2])
    low = after(low + swapped(give_low), part)
    up = after(up + swapped(give_up), part)
    above = from_tile(low, -1)
    below = from_tile(up, 1)
    part = summed_over(summed_one_way(part), TILE[1])
    up, low, above, below = lax.optimization_barrier((up, low, above, below))
    own_half = updated(up + above, in_blocks(own_half))
    mine = jnp.concatenate([own_half, updated(low + below, in_blocks(halo))], axis=2)
    other = swapped(mine)
    probe_field = next_probe(after(part, mine), None, probe_field)
    up, low, give_up, give_low, keep_sums, give_sums = run_positions(
        scalars, probe_field, amps, tables, None, mine, other
    )
    part = scattered_over(keep_sums + swapped(give_sums), TILE[2])
    low = after(low + swapped(give_low), part)
    up = up + swapped(give_up)
    above = from_tile(low, -1)
    part = summed_over(summed_one_way(part), TILE[1])
    up = after(up, part)
    mine = updated(up + above, own_half).transpose(0, 2, 1, 3).reshape(2, STRIP, COLS // 2)
    other = swapped(mine)
    left = jnp.where(core == 0, mine, other)
    right = jnp.where(core == 0, other, mine)
    object_out = jnp.concatenate([left, right], axis=2)
    probe_out = next_probe(part, object_out, probe_field)
    return object_out, probe_out


def torus_of(mesh):
    shape = (mesh.shape["tile"],)
    shape = (8, 4, 4) if shape == (128,) else (1, 1, *shape)
    return Mesh(mesh.devices.reshape(*shape, mesh.shape["pos"]), (*TILE, "pos"))


def solution(mesh):
    return jax.shard_map(
        on_device,
        mesh=torus_of(mesh),
        in_specs=(
            P(None, TILE, None),
            P(),
            P(TILE, "pos", None, None, None),
            P(TILE, "pos", None),
            P(TILE, "pos", None),
            P(TILE, "pos"),
        ),
        out_specs=(P(None, TILE, None), P()),
        check_vma=False,
    )
```
